128 devices in a mesh: wide: 32 (over z_hi, x, y), narrow: 4 (over z_lo, core).
Axes of the slice: x: 4, y: 4, z: 4 (z_hi: 2, z_lo: 2; z = z_hi * 2 + z_lo), core: 2. Of those that a mesh axis runs over, the one named last changes fastest.
Arguments:
- activations: bfloat16 [16, 2560, 768], P('narrow', 'wide'), may hold values from -6 to 6
- conditioning: bfloat16 [16, 2560, 384], P('narrow', 'wide'), may hold values from -6 to 6
- pair_features: bfloat16 [2560, 2560, 128], P('wide', 'narrow'), may hold values from -6 to 6
- key_mask: int32 [2560], P('wide'), may hold values from 0 to 1, as said below
- w_scale: bfloat16 [384, 768], replicated, may hold values from -0.3125 to 0.3125
- w_shift: bfloat16 [384, 768], replicated, may hold values from -0.3125 to 0.3125
- w_query: bfloat16 [768, 768], replicated, may hold values from -0.21875 to 0.21875
- w_key: bfloat16 [768, 768], replicated, may hold values from -0.21875 to 0.21875
- w_value: bfloat16 [768, 768], replicated, may hold values from -0.21875 to 0.21875
- w_gate: bfloat16 [768, 768], replicated, may hold values from -0.21875 to 0.21875
- w_out: bfloat16 [768, 768], replicated, may hold values from -0.21875 to 0.21875
- w_outgate: bfloat16 [384, 768], replicated, may hold values from -0.3125 to 0.3125
- w_bias: bfloat16 [128, 16], replicated, may hold values from -9 to 9
Outputs:
- updated: bfloat16 [16, 2560, 768], P('narrow', 'wide')
The draws below stay inside these ranges and needn't reach their ends.
Inputs may be any that keep to these rules, and one draw needn't show every extreme that they name: key_mask is 1 on the first token of every aligned block of 80 tokens and 0 on the last of the 2560 tokens; every other token is 0 or 1 independently.
All inputs are finite; a program needn't handle non-finite values.
Results may differ from the reference program's by a relative error of at most 0.0049.
Values may be sent and summed in bfloat16 or wider, within the bound.
No kernel may reach another device: no remote copies, remote signals or barrier semaphores. Data moves between devices by JAX's collectives and lax.ppermute only.
A program may use at most 192 MiB of HBM per device.

```python
import math
import jax
import jax.numpy as jnp
from jax import lax

D = 768
H = 16
C = 128
CS = 384
TOK_DEV = 80
TOKENS = 2560
SAMPLES = 16
N_WIDE = 32


def bias_entries(key, highest):
    key = jax.random.fold_in(key, 11)
    order_key, entry_key = jax.random.split(key)
    ladder = jnp.exp(jnp.linspace(math.log(0.3), math.log(highest), H))
    order = jax.random.permutation(order_key, H)
    spread = ladder[order]
    entries = jnp.clip(jax.random.normal(entry_key, (C, H), jnp.float32), -4.0, 4.0)
    return (entries, spread)


def draw_w_bias(key, part):
    highest = 3.0
    entries, spread = bias_entries(key, highest)
    return jnp.clip(entries * spread[None, :] / math.sqrt(C), -9.0, 9.0).astype(jnp.bfloat16)


def draw_pair_features(key, part):
    key = jax.random.fold_in(key, 13)
    values = jnp.clip(jax.random.normal(key, (TOKENS, TOKENS, C), jnp.float32), -6.0, 6.0)
    return values.astype(jnp.bfloat16)


def draw_activations(key, part):
    key = jax.random.fold_in(key, 5)
    common_key, rough_key = jax.random.split(key)
    common = jnp.clip(1.2 * jax.random.normal(common_key, (SAMPLES, 1, D), jnp.float32), -3.5, 3.5)
    rough = jnp.clip(0.8 * jax.random.normal(rough_key, (SAMPLES, TOKENS, D), jnp.float32), -2.5, 2.5)
    return jnp.clip(common + rough, -6.0, 6.0).astype(jnp.bfloat16)


def draw_key_mask(key, part):
    key = jax.random.fold_in(key, 7)
    rolled = jax.random.randint(key, (TOKENS,), 0, 8)
    position = jnp.arange(TOKENS)
    flags = (rolled > 0).astype(jnp.int32)
    flags = jnp.where(position % TOK_DEV == 0, 1, flags)
    flags = jnp.where(position == TOKENS - 1, 0, flags)
    return flags.astype(jnp.int32)


def block_scale(key, dims, cuts, low, top_value):
    factor_of, own = 1.0, jax.random.fold_in(key, 6)
    for dim, blocks in cuts:
        draws = jnp.exp(jax.random.uniform(jax.random.fold_in(own, dim), (blocks,), jnp.float32, low / len(cuts), top_value / len(cuts)))
        factor_of = factor_of * jnp.repeat(draws, dims[dim] // blocks).reshape([-1 if axis == dim else 1 for axis in range(len(dims))])
    return factor_of


def centred(own_key, extent, deviation, most, pieces=(), kind=jnp.bfloat16):
    level = block_scale(own_key, extent, pieces, -0.22, 0.18) if pieces else 1.0
    values = jax.random.normal(own_key, extent, jnp.float32) * deviation * level
    return jnp.minimum(jnp.maximum(values, -most), most).astype(kind)


def setup_inputs(seed: int = 0) -> dict:
    seeds = jax.random.split(jax.random.key(seed), 14)
    return {
        "activations": draw_activations(jax.random.fold_in(seeds[13], 71), 0),
        "conditioning": centred(seeds[1], (SAMPLES, TOKENS, CS), 1.0, 6.0, ((0, 4), (1, 32))),
        "pair_features": draw_pair_features(jax.random.fold_in(seeds[13], 71), 0),
        "key_mask": draw_key_mask(jax.random.fold_in(seeds[13], 71), 0),
        "w_scale": centred(seeds[4], (CS, D), CS ** -0.5, 0.3125),
        "w_shift": centred(seeds[5], (CS, D), CS ** -0.5, 0.3125),
        "w_query": centred(seeds[6], (D, D), D ** -0.5, 0.21875),
        "w_key": centred(seeds[7], (D, D), D ** -0.5, 0.21875),
        "w_value": centred(seeds[8], (D, D), D ** -0.5, 0.21875),
        "w_gate": centred(seeds[9], (D, D), D ** -0.5, 0.21875),
        "w_out": centred(seeds[10], (D, D), D ** -0.5, 0.21875),
        "w_outgate": centred(seeds[11], (CS, D), CS ** -0.5, 0.3125),
        "w_bias": draw_w_bias(jax.random.fold_in(seeds[13], 71), 0),
    }


EPSILON = 1e-05
NEGATIVE = -1e+30

def layer_norm(entries):
    entries = entries.astype(jnp.float32)
    row_mean = lax.optimization_barrier(jnp.mean(entries, axis=-1, keepdims=True))
    centered = entries - row_mean
    variance = lax.optimization_barrier(jnp.mean(centered * centered, axis=-1, keepdims=True))
    return centered * lax.rsqrt(variance + EPSILON)

def widen(entries):
    return lax.optimization_barrier(entries).astype(jnp.float32)

def project(rows_in, weight):
    return jnp.dot(rows_in, weight, preferred_element_type=jnp.float32)

def reference(activations, conditioning, pair_features, key_mask, w_scale, w_shift, w_query, w_key, w_value, w_gate, w_out, w_outgate, w_bias):
    score_scale = 1.0 / math.sqrt(D // H)

    def bias_rows(row_block):
        pair_norm = layer_norm(row_block).astype(jnp.bfloat16)
        return jnp.einsum('ijc,ch->hij', widen(pair_norm), w_bias.astype(jnp.float32)).astype(jnp.bfloat16)
    blocks = lax.map(bias_rows, pair_features.reshape(N_WIDE, TOK_DEV, TOKENS, C))
    pair_bias = jnp.transpose(blocks, (1, 0, 2, 3)).reshape(H, TOKENS, TOKENS)
    cond_norm = layer_norm(conditioning).astype(jnp.bfloat16)
    modulated = (jax.nn.sigmoid(project(cond_norm, w_scale)) * layer_norm(activations) + project(cond_norm, w_shift)).astype(jnp.bfloat16)
    queries = project(modulated, w_query).astype(jnp.bfloat16).reshape(SAMPLES, TOKENS, H, D // H)
    key_rows = project(modulated, w_key).astype(jnp.bfloat16).reshape(SAMPLES, TOKENS, H, D // H)
    value_rows = project(modulated, w_value).astype(jnp.bfloat16).reshape(SAMPLES, TOKENS, H, D // H)
    gate_rows = jax.nn.sigmoid(project(modulated, w_gate))
    visible = key_mask[None, None, :] > 0
    bias_wide = widen(pair_bias)

    def one_sample(item):
        sample_queries, sample_keys, sample_values = item
        scores = jnp.einsum('qhd,khd->hqk', widen(sample_queries), widen(sample_keys))
        scores = scores * score_scale + bias_wide
        scores = jnp.where(visible, scores, NEGATIVE)
        row_top = lax.optimization_barrier(jnp.max(scores, axis=2, keepdims=True))
        exponent = jnp.exp(scores - row_top)
        probabilities = (exponent / lax.optimization_barrier(jnp.sum(exponent, axis=2, keepdims=True))).astype(jnp.bfloat16)
        return jnp.einsum('hqk,khd->qhd', widen(probabilities), widen(sample_values))
    attended = lax.map(one_sample, (queries, key_rows, value_rows)).reshape(SAMPLES, TOKENS, D)
    gated = (gate_rows * attended).astype(jnp.bfloat16)
    out_gate = jax.nn.sigmoid(project(cond_norm, w_outgate))
    return (activations.astype(jnp.float32) + out_gate * project(gated, w_out)).astype(jnp.bfloat16)
```

```python
import math

import jax
import jax.numpy as jnp
import numpy as np
from jax import lax
from jax.experimental import pallas as pl
from jax.experimental.pallas import tpu as pltpu
from jax.sharding import Mesh, PartitionSpec as P

EPSILON = 1e-05
NEGATIVE = -1e30
LOG2E = math.log2(math.e)
HEADS = 16
HEAD = 48
LANES = 128
GROUP = 8
XZ = ("zh", "x", "zl")
BF = jnp.bfloat16
F32 = jnp.float32
VMEM_BYTES = 56 * 1024 * 1024
NT = (((1,), (1,)), ((), ()))


def layer_norm(entries):
    entries = entries.astype(F32)
    row_mean = jnp.mean(entries, axis=-1, keepdims=True)
    centered = entries - row_mean
    variance = jnp.mean(centered * centered, axis=-1, keepdims=True)
    return centered * lax.rsqrt(variance + EPSILON)


def dot(left, right):
    return jnp.dot(left, right, preferred_element_type=F32)


def placement():
    table = np.zeros((2, GROUP, HEAD, GROUP, 2, 64), np.float32)
    for head in range(GROUP):
        for channel in range(HEAD):
            table[0, head, channel, head, 0, channel] = 1
            table[1, head, channel, head, 1, channel] = 1
    return jnp.asarray(table.reshape(2 * GROUP * HEAD, GROUP * LANES), BF)


def qkv_kernel(act, cond, extra, place, ws, wsh, wq, wk, wv, kv_out, q_out, mod_out, cn_out, mod):
    samples, tokens, width = act.shape
    rows = samples * tokens

    @pl.when(pl.program_id(0) == 0)
    def _():
        cond_norm = layer_norm(cond[...].reshape(rows, cond.shape[2])).astype(BF)
        normed = layer_norm(act[...].reshape(rows, width))
        modulated = jax.nn.sigmoid(dot(cond_norm, ws[...])) * normed + dot(cond_norm, wsh[...])
        mod[...] = modulated.astype(BF)
        mod_out[...] = mod[...].reshape(mod_out.shape)
        cn_out[...] = cond_norm.reshape(cn_out.shape)

    modulated = mod[...]
    q = (dot(modulated, wq[...]) * (LOG2E / math.sqrt(HEAD))).astype(BF)
    k = dot(modulated, wk[...]).astype(BF)
    v = dot(modulated, wv[...]).astype(BF)
    table = place[...]
    for s in range(samples):
        row = slice(s * tokens, (s + 1) * tokens)
        pair = [k[row], v[row]] if s % 2 == 0 else [v[row], k[row]]
        placed = dot(jnp.concatenate(pair, axis=1), table).astype(BF)
        for h in range(GROUP):
            kv_out[h, s] = placed[:, h * LANES:(h + 1) * LANES] + extra[s % 2]
    lane = lax.broadcasted_iota(jnp.int32, (tokens, LANES), 1)
    one = jnp.where((lane == HEAD) | (lane == 64 + HEAD), 1.0, 0.0).astype(BF)
    for p in range(samples // 2):
        first = slice(2 * p * tokens, (2 * p + 1) * tokens)
        second = slice((2 * p + 1) * tokens, (2 * p + 2) * tokens)
        placed = dot(jnp.concatenate([q[first], q[second]], axis=1), table).astype(BF)
        for h in range(GROUP):
            q_out[h, p] = placed[:, h * LANES:(h + 1) * LANES] + one


def project_qkv(act, cond, extra, place, ws, wsh, wq, wk, wv):
    samples, tokens, width = act.shape
    steps = HEADS // GROUP
    columns = GROUP * HEAD
    whole = lambda a: pl.BlockSpec(a.shape, lambda g: (0,) * a.ndim)
    part = pl.BlockSpec((width, columns), lambda g: (0, g))
    return pl.pallas_call(
        qkv_kernel,
        grid=(steps,),
        in_specs=[whole(act), whole(cond), whole(extra), whole(place), whole(ws), whole(wsh), part, part, part],
        out_specs=[
            pl.BlockSpec((GROUP, samples, tokens, LANES), lambda g: (g, 0, 0, 0)),
            pl.BlockSpec((GROUP, samples // 2, tokens, LANES), lambda g: (g, 0, 0, 0)),
            whole(act),
            whole(cond),
        ],
        out_shape=[
            jax.ShapeDtypeStruct((HEADS, samples, tokens, LANES), BF),
            jax.ShapeDtypeStruct((HEADS, samples // 2, tokens, LANES), BF),
            jax.ShapeDtypeStruct(act.shape, BF),
            jax.ShapeDtypeStruct(cond.shape, BF),
        ],
        scratch_shapes=[pltpu.VMEM((samples * tokens, width), BF)],
        compiler_params=pltpu.CompilerParams(vmem_limit_bytes=VMEM_BYTES),
        cost_estimate=pl.CostEstimate(flops=4_000_000_000, bytes_accessed=10_000_000, transcendentals=300_000),
        name="qkv",
    )(act, cond, extra, place, ws, wsh, wq, wk, wv)


def bias_kernel(pair, weights, sums, out, rows):
    count = pair.shape[0]
    mean_table = jnp.full((LANES, LANES), 1.0 / LANES, BF)
    for i in range(count):
        x = pair[i]
        c = x - dot(x, mean_table).astype(BF)
        both = jnp.concatenate([c, c * c], axis=1)
        r = lax.dot_general(weights[...], both, NT, preferred_element_type=F32)
        shift = r[HEADS:HEADS + 1]
        scale = lax.rsqrt(r[HEADS + 8:HEADS + 9] - shift * shift + EPSILON) * LOG2E
        rows[i] = (r[:HEADS] - shift * sums[...]) * scale
    out[...] = jnp.swapaxes(rows[...], 0, 1).astype(BF)


def project_bias(pair, w_bias):
    queries, keys, channels = pair.shape
    step = 16
    wt = w_bias.T
    zero = jnp.zeros((HEADS, channels), BF)
    part = jnp.full((8, channels), 1.0 / channels, BF)
    weights = jnp.concatenate(
        [
            jnp.concatenate([wt, zero], axis=1),
            jnp.concatenate([part, zero[:8]], axis=1),
            jnp.concatenate([zero[:8], part], axis=1),
        ],
        axis=0,
    )
    sums = jnp.sum(wt.astype(F32), axis=1, keepdims=True)
    return pl.pallas_call(
        bias_kernel,
        grid=(queries // step,),
        in_specs=[
            pl.BlockSpec((step, keys, channels), lambda i: (i, 0, 0)),
            pl.BlockSpec(weights.shape, lambda i: (0, 0)),
            pl.BlockSpec(sums.shape, lambda i: (0, 0)),
        ],
        out_specs=pl.BlockSpec((HEADS, step, keys), lambda i: (0, i, 0)),
        out_shape=jax.ShapeDtypeStruct((HEADS, queries, keys), BF),
        scratch_shapes=[pltpu.VMEM((step, HEADS, keys), F32)],
        compiler_params=pltpu.CompilerParams(vmem_limit_bytes=VMEM_BYTES),
        cost_estimate=pl.CostEstimate(flops=10_000_000_000, bytes_accessed=15_000_000, transcendentals=100_000),
        name="bias",
    )(pair, weights, sums)


T = 4


def attend_kernel(core, q, kv, own, other, out, keys):
    tokens = q.shape[3]
    me = core[0]
    for z in range(2):
        for o in range(2):
            quarter = me if o == 0 else 1 - me
            for low in range(2):
                for y in range(4):
                    at = ((z * 2 + o) * 8 + low * 4 + y) * tokens
                    for s in range(2):
                        keys[s, at:at + tokens] = kv[y, z, 2 * quarter + low, 0, s]
    span = T * tokens
    lane = lax.broadcasted_iota(jnp.int32, (span, LANES), 1)
    low_half = lane < 64

    def block(t, carry):
        pair_q = q[pl.ds(t * T, T), 0, 0].reshape(span, LANES)
        results = []
        for s in range(2):
            mine = jnp.where(low_half if s == 0 else ~low_half, pair_q, jnp.zeros_like(pair_q))
            scores = []
            for z in range(2):
                for o in range(2):
                    at = (z * 2 + o) * 8 * tokens
                    b = (own if o == 0 else other)[pl.ds(t * T, T), z].reshape(span, 8 * tokens)
                    part = lax.dot_general(mine, keys[s, at:at + 8 * tokens], NT, preferred_element_type=F32)
                    scores.append(part + b.astype(F32))
            tops = [jnp.max(part, axis=1, keepdims=True) for part in scores]
            top = jnp.maximum(jnp.maximum(tops[0], tops[1]), jnp.maximum(tops[2], tops[3]))
            total = None
            for n, part in enumerate(scores):
                p = jnp.exp2(part - top).astype(BF)
                o_part = dot(p, keys[s, n * 8 * tokens:(n + 1) * 8 * tokens])
                total = o_part if total is None else total + o_part
            at = 64 + HEAD if s == 0 else HEAD
            results.append(total / total[:, at:at + 1])
        merged = jnp.where(low_half, results[1], results[0]).astype(BF)
        out[pl.ds(t * T, T), 0, 0] = merged.reshape(T, tokens, LANES)
        return carry

    lax.fori_loop(0, 8 // T, block, 0)


def attend(core, q, kv, own, other):
    tokens = q.shape[3]
    q_spec = pl.BlockSpec((8, 1, 1, tokens, LANES), lambda z, p, c: (0, z, p, 0, 0))
    b_spec = pl.BlockSpec(own.shape, lambda z, p, c: (0, 0, 0, 0))
    return pl.pallas_call(
        attend_kernel,
        grid_spec=pltpu.PrefetchScalarGridSpec(
            num_scalar_prefetch=1,
            grid=(2, 2),
            in_specs=[
                q_spec,
                pl.BlockSpec((4, 2, 4, 1, 2, tokens, LANES), lambda z, p, c: (0, 0, 0, z, p, 0, 0)),
                b_spec,
                b_spec,
            ],
            out_specs=q_spec,
            scratch_shapes=[pltpu.VMEM((2, 32 * tokens, LANES), BF)],
        ),
        out_shape=jax.ShapeDtypeStruct(q.shape, BF),
        compiler_params=pltpu.CompilerParams(vmem_limit_bytes=VMEM_BYTES),
        cost_estimate=pl.CostEstimate(flops=14_000_000_000, bytes_accessed=10_000_000, transcendentals=13_000_000),
        name="attend",
    )(core, q, kv, own, other)


def gate_kernel(mod, cn, place, wg, wog, gate_out, og_out):
    samples, tokens, width = mod.shape
    rows = samples * tokens
    og_out[...] = jax.nn.sigmoid(dot(cn[...].reshape(rows, cn.shape[2]), wog[...])).reshape(og_out.shape)
    columns = GROUP * HEAD
    low = place[0:columns]
    high = place[columns:2 * columns]
    for g in range(HEADS // GROUP):
        w = wg[:, g * columns:(g + 1) * columns]
        w_low = dot(w, low).astype(BF)
        w_high = dot(w, high).astype(BF)
        for p in range(samples // 2):
            value = dot(mod[2 * p + 1], w_low) + dot(mod[2 * p], w_high)
            gate_out[p, :, g * GROUP * LANES:(g + 1) * GROUP * LANES] = jax.nn.sigmoid(value)


def gates(mod, cn, place, wg, wog):
    samples, tokens, width = mod.shape
    return pl.pallas_call(
        gate_kernel,
        out_shape=[
            jax.ShapeDtypeStruct((samples // 2, tokens, HEADS * LANES), F32),
            jax.ShapeDtypeStruct(mod.shape, F32),
        ],
        compiler_params=pltpu.CompilerParams(vmem_limit_bytes=VMEM_BYTES),
        cost_estimate=pl.CostEstimate(flops=4_000_000_000, bytes_accessed=9_000_000, transcendentals=1_000_000),
        name="gates",
    )(mod, cn, place, wg, wog)


def out_kernel(attended, gate, og, act, wo, out, low, high):
    samples, tokens, width = act.shape
    low[...] = jnp.zeros_like(low)
    high[...] = jnp.zeros_like(high)
    for h in range(HEADS):
        rows = wo[h * HEAD:(h + 1) * HEAD]
        low[h * LANES:h * LANES + HEAD] = rows
        high[h * LANES + 64:h * LANES + 64 + HEAD] = rows
    for p in range(samples // 2):
        gated = jnp.concatenate(
            [
                (attended[h, p].astype(F32) * gate[p, :, h * LANES:(h + 1) * LANES]).astype(BF)
                for h in range(HEADS)
            ],
            axis=1,
        )
        for s, table in ((2 * p, high), (2 * p + 1, low)):
            out[s] = (act[s].astype(F32) + og[s] * dot(gated, table[...])).astype(BF)


def project_out(attended, gate, og, act, wo):
    width = act.shape[2]
    return pl.pallas_call(
        out_kernel,
        out_shape=jax.ShapeDtypeStruct(act.shape, BF),
        scratch_shapes=[pltpu.VMEM((HEADS * LANES, width), BF)] * 2,
        compiler_params=pltpu.CompilerParams(vmem_limit_bytes=VMEM_BYTES),
        cost_estimate=pl.CostEstimate(flops=2_000_000_000, bytes_accessed=6_000_000, transcendentals=0),
        name="out",
    )(attended, gate, og, act, wo)


def key_extras(key_mask):
    pad = jnp.where(key_mask > 0, 0.0, NEGATIVE)[:, None]
    lane = jnp.arange(LANES)[None, :]
    first = jnp.where(lane == HEAD, pad, jnp.where(lane == 64 + HEAD, 1.0, 0.0))
    second = jnp.where(lane == 64 + HEAD, pad, jnp.where(lane == HEAD, 1.0, 0.0))
    return jnp.stack([first, second]).astype(BF)


def per_device(
    activations,
    conditioning,
    pair_features,
    key_mask,
    w_scale,
    w_shift,
    w_query,
    w_key,
    w_value,
    w_gate,
    w_out,
    w_outgate,
    w_bias,
):
    tokens = activations.shape[1]
    place = placement()
    kv, q, modulated, cond_norm = project_qkv(
        activations, conditioning, key_extras(key_mask), place, w_scale, w_shift, w_query, w_key, w_value
    )
    exchange = lambda a: lax.all_to_all(a, XZ, 0, 0, tiled=True)
    kv = exchange(kv)
    kv = lax.all_gather(kv, "y", axis=0)
    q = exchange(q)
    own = exchange(project_bias(pair_features, w_bias))
    other = lax.ppermute(own, "co", [(0, 1), (1, 0)])
    gate, out_gate = gates(modulated, cond_norm, place, w_gate, w_outgate)
    core = lax.axis_index("co").astype(jnp.int32).reshape(1)
    keys = own.shape[2]
    attended = attend(
        core,
        q.reshape(8, 2, 2, tokens, LANES),
        kv.reshape(4, 2, 4, 2, 4, tokens, LANES),
        own.reshape(8, 2, tokens, keys),
        other.reshape(8, 2, tokens, keys),
    )
    attended = exchange(attended.reshape(HEADS, 2, tokens, LANES))
    return project_out(attended, gate, out_gate, activations, w_out)


def solution(mesh):
    fine = Mesh(mesh.devices.reshape(2, 4, 4, 2, 2), ("zh", "x", "y", "zl", "co"))
    wide, narrow = ("zh", "x", "y"), ("zl", "co")
    in_specs = (
        P(narrow, wide, None),
        P(narrow, wide, None),
        P(wide, narrow, None),
        P(wide),
    ) + (P(),) * 9
    return jax.shard_map(
        per_device, mesh=fine, in_specs=in_specs, out_specs=P(narrow, wide, None), check_vma=False
    )
```

```python
import math

import jax
import jax.numpy as jnp
import numpy as np
from jax import lax
from jax.experimental import pallas as pl
from jax.experimental.pallas import tpu as pltpu
from jax.sharding import Mesh, PartitionSpec as P

EPSILON = 1e-05
NEGATIVE = -1e30
LOG2E = math.log2(math.e)
HEADS = 16
HEAD = 48
LANES = 128
GROUP = 8
MARK_LANE = 95
PAD_LANE = 96
SUM_LANE = 97
XZ = ("zh", "x", "zl")
BF = jnp.bfloat16
F32 = jnp.float32
VMEM_BYTES = 56 * 1024 * 1024
NT = (((1,), (1,)), ((), ()))


def layer_norm(entries):
    entries = entries.astype(F32)
    row_mean = jnp.mean(entries, axis=-1, keepdims=True)
    centered = entries - row_mean
    variance = jnp.mean(centered * centered, axis=-1, keepdims=True)
    return centered * lax.rsqrt(variance + EPSILON)


def dot(left, right):
    return jnp.dot(left, right, preferred_element_type=F32)


def placement():
    table = np.zeros((2, 2, GROUP, HEAD, GROUP, LANES), np.float32)
    for head in range(GROUP):
        for channel in range(HEAD):
            for which, offset in ((0, HEAD), (1, 64)):
                table[which, 0, head, channel, head, channel] = 1
                table[which, 1, head, channel, head, offset + channel] = 1
    table = table.reshape(2, 2 * GROUP * HEAD, GROUP * LANES)
    return jnp.asarray(table[0], BF), jnp.asarray(table[1], BF)


def qkv_kernel(act, cond, mask, kv_place, q_place, ws, wsh, wq, wk, wv, kv_out, q_out, mod_out, cn_out, mod):
    samples, tokens, width = act.shape
    rows = samples * tokens

    @pl.when(pl.program_id(0) == 0)
    def _():
        cond_norm = layer_norm(cond[...].reshape(rows, cond.shape[2])).astype(BF)
        normed = layer_norm(act[...].reshape(rows, width))
        modulated = jax.nn.sigmoid(dot(cond_norm, ws[...])) * normed + dot(cond_norm, wsh[...])
        mod[...] = modulated.astype(BF)
        mod_out[...] = mod[...].reshape(mod_out.shape)
        cn_out[...] = cond_norm.reshape(cn_out.shape)

    modulated = mod[...]
    k = dot(modulated, wk[...]).astype(BF)
    v = dot(modulated, wv[...]).astype(BF)
    placed = dot(jnp.concatenate([k, v], axis=1), kv_place[...])
    lane = lax.broadcasted_iota(jnp.int32, (tokens, LANES), 1)
    square = (tokens, tokens)
    diagonal = lax.broadcasted_iota(jnp.int32, square, 0) == lax.broadcasted_iota(jnp.int32, square, 1)
    padded = jnp.broadcast_to(jnp.where(mask[...] > 0, 0.0, 1.0), square)
    padded = jnp.sum(jnp.where(diagonal, padded, 0.0), axis=1, keepdims=True)
    marked = (lane == MARK_LANE) & (padded > 0.5)
    for h in range(GROUP):
        tile = placed[:, h * LANES:(h + 1) * LANES]
        last = tile[3 * tokens:]
        for s in range(3):
            spare = pltpu.roll(last, 96 - 32 * s, axis=1)
            merged = jnp.where(lane < 96, tile[s * tokens:(s + 1) * tokens], spare)
            if s == 0:
                merged = jnp.where(marked, NEGATIVE, merged)
            kv_out[h, :, s * LANES:(s + 1) * LANES] = merged.astype(BF)
    q = (dot(modulated, wq[...]) * (LOG2E / math.sqrt(HEAD))).astype(BF)
    first = jnp.concatenate([q[:tokens], q[2 * tokens:3 * tokens]], axis=0)
    second = jnp.concatenate([q[tokens:2 * tokens], q[3 * tokens:]], axis=0)
    placed = dot(jnp.concatenate([first, second], axis=1), q_place[...]).astype(BF)
    for p in range(samples // 2):
        for h in range(GROUP):
            q_out[h, :, p * LANES:(p + 1) * LANES] = placed[p * tokens:(p + 1) * tokens, h * LANES:(h + 1) * LANES]


def project_qkv(act, cond, mask, kv_place, q_place, ws, wsh, wq, wk, wv):
    samples, tokens, width = act.shape
    steps = HEADS // GROUP
    columns = GROUP * HEAD
    whole = lambda a: pl.BlockSpec(a.shape, lambda g: (0,) * a.ndim)
    part = pl.BlockSpec((width, columns), lambda g: (0, g))
    return pl.pallas_call(
        qkv_kernel,
        grid=(steps,),
        in_specs=[whole(act), whole(cond), whole(mask), whole(kv_place), whole(q_place), whole(ws), whole(wsh), part, part, part],
        out_specs=[
            pl.BlockSpec((GROUP, tokens, 3 * LANES), lambda g: (g, 0, 0)),
            pl.BlockSpec((GROUP, tokens, 2 * LANES), lambda g: (g, 0, 0)),
            whole(act),
            whole(cond),
        ],
        out_shape=[
            jax.ShapeDtypeStruct((HEADS, tokens, 3 * LANES), BF),
            jax.ShapeDtypeStruct((HEADS, tokens, 2 * LANES), BF),
            jax.ShapeDtypeStruct(act.shape, BF),
            jax.ShapeDtypeStruct(cond.shape, BF),
        ],
        scratch_shapes=[pltpu.VMEM((samples * tokens, width), BF)],
        compiler_params=pltpu.CompilerParams(vmem_limit_bytes=VMEM_BYTES),
        cost_estimate=pl.CostEstimate(flops=4_000_000_000, bytes_accessed=10_000_000, transcendentals=300_000),
        name="qkv",
    )(act, cond, mask, kv_place, q_place, ws, wsh, wq, wk, wv)


def bias_kernel(pair, w_bias, q, out, rows):
    count, keys, channels = pair.shape
    wt = w_bias[...].astype(F32).T.astype(BF)
    zero = jnp.zeros((HEADS, channels), BF)
    part = jnp.full((HEADS, channels), 1.0 / channels, BF)
    weights = jnp.concatenate(
        [jnp.concatenate([wt, zero], axis=1), jnp.concatenate([zero, part], axis=1)], axis=0
    )
    for i in range(count):
        x = pair[i].astype(F32)
        c = (x - jnp.mean(x, axis=1, keepdims=True)).astype(BF)
        both = jnp.concatenate([c, c * c], axis=1)
        r = lax.dot_general(weights, both, NT, preferred_element_type=F32)
        rows[i] = r[:HEADS] * (lax.rsqrt(r[HEADS:] + EPSILON) * LOG2E)
    out[:, :, :keys] = jnp.swapaxes(rows[...], 0, 1).astype(BF)
    out[:, :, keys:] = q[...]


def project_bias(pair, w_bias, q):
    queries, keys, channels = pair.shape
    step = 16
    extent = keys + q.shape[2]
    return pl.pallas_call(
        bias_kernel,
        grid=(queries // step,),
        in_specs=[
            pl.BlockSpec((step, keys, channels), lambda i: (i, 0, 0)),
            pl.BlockSpec(w_bias.shape, lambda i: (0, 0)),
            pl.BlockSpec((HEADS, step, q.shape[2]), lambda i: (0, i, 0)),
        ],
        out_specs=pl.BlockSpec((HEADS, step, extent), lambda i: (0, i, 0)),
        out_shape=jax.ShapeDtypeStruct((HEADS, queries, extent), BF),
        scratch_shapes=[pltpu.VMEM((step, HEADS, keys), F32)],
        compiler_params=pltpu.CompilerParams(vmem_limit_bytes=VMEM_BYTES),
        cost_estimate=pl.CostEstimate(flops=10_000_000_000, bytes_accessed=15_000_000, transcendentals=100_000),
        name="bias",
    )(pair, w_bias, q)


T = 4


def attend_kernel(core, q, kv, own, other, out, keys):
    tokens = q.shape[2]
    chunk = 8 * tokens
    me = core[0]
    lane_k = lax.broadcasted_iota(jnp.int32, (tokens, LANES), 1)

    @pl.when(pl.program_id(1) == 0)
    def _():
        for z in range(2):
            for o in range(2):
                quarter = me if o == 0 else 1 - me
                for low in range(2):
                    for y in range(4):
                        block = low * 4 + y
                        at = (z * 2 + o) * chunk + block * tokens
                        tiles = [kv[y, z, 2 * quarter + low, 0, :, i * LANES:(i + 1) * LANES] for i in range(3)]
                        wide = [t.astype(F32) for t in tiles]
                        pad = jnp.where(pltpu.roll(wide[0], PAD_LANE - MARK_LANE, axis=1) < 0.5 * NEGATIVE, NEGATIVE, 0.0)
                        tail = jnp.where(lane_k == PAD_LANE, pad, jnp.where(lane_k == SUM_LANE, 1.0, 0.0)).astype(BF)
                        for s in range(3):
                            keys[s, at:at + tokens] = jnp.where(lane_k < 96, tiles[s], tail)
                        last = jnp.where(
                            lane_k < 32,
                            pltpu.roll(wide[0], 32, axis=1),
                            jnp.where(lane_k < 64, pltpu.roll(wide[1], 64, axis=1), pltpu.roll(wide[2], 96, axis=1)),
                        ).astype(BF)
                        keys[3, at:at + tokens] = jnp.where(lane_k < 96, last, tail)

    first_sample = 2 * pl.program_id(1)
    span = T * tokens
    lane = lax.broadcasted_iota(jnp.int32, (span, LANES), 1)
    pad_one = jnp.where(lane == PAD_LANE, 1.0, 0.0).astype(BF)
    blocks = [(t, s) for t in range(8 // T) for s in range(2)]

    def scores_of(t, s, c):
        pair_q = q[t * T:(t + 1) * T, 0].reshape(span, LANES)
        if s == 1:
            pair_q = pltpu.roll(pair_q.astype(F32), 64, axis=1).astype(BF)
        mine = jnp.where(lane < HEAD, pair_q, pad_one)
        part = lax.dot_general(
            mine, keys[first_sample + s, c * chunk:(c + 1) * chunk], NT, preferred_element_type=F32
        )
        b = (own if c % 2 == 0 else other)[t * T:(t + 1) * T, c // 2].reshape(span, chunk)
        return part + b.astype(F32)

    current = [scores_of(*blocks[0], c) for c in range(4)]
    for i, (t, s) in enumerate(blocks):
        tops = [jnp.max(part, axis=1, keepdims=True) for part in current]
        top = jnp.maximum(jnp.maximum(tops[0], tops[1]), jnp.maximum(tops[2], tops[3]))
        following, total = [], None
        for c in range(4):
            if i + 1 < len(blocks):
                following.append(scores_of(*blocks[i + 1], c))
            p = jnp.exp2(current[c] - top).astype(BF)
            part = dot(p, keys[first_sample + s, c * chunk:(c + 1) * chunk])
            total = part if total is None else total + part
        current = following
        result = total / total[:, SUM_LANE:SUM_LANE + 1]
        if s == 0:
            low = pltpu.roll(result, LANES - HEAD, axis=1)
        else:
            high = pltpu.roll(result, 64 - HEAD, axis=1)
            merged = jnp.where(lane < 64, low, high).astype(BF)
            out[t * T:(t + 1) * T, 0] = merged.reshape(T, tokens, LANES)


def attend(core, kv, own, other):
    tokens = own.shape[2]
    chunk = 8 * tokens
    b_spec = pl.BlockSpec((8, 2, tokens, chunk), lambda z, p, c: (0, 0, 0, 0))
    return pl.pallas_call(
        attend_kernel,
        grid_spec=pltpu.PrefetchScalarGridSpec(
            num_scalar_prefetch=1,
            grid=(2, 2),
            in_specs=[
                pl.BlockSpec((8, 1, tokens, LANES), lambda z, p, c: (0, z, 0, chunk // LANES + p)),
                pl.BlockSpec((4, 2, 4, 1, tokens, 3 * LANES), lambda z, p, c: (0, 0, 0, z, 0, 0)),
                b_spec,
                b_spec,
            ],
            out_specs=pl.BlockSpec((8, 1, tokens, LANES), lambda z, p, c: (0, z, 0, p)),
            scratch_shapes=[pltpu.VMEM((4, 4 * chunk, LANES), BF)],
        ),
        out_shape=jax.ShapeDtypeStruct((8, 2, tokens, 2 * LANES), BF),
        compiler_params=pltpu.CompilerParams(vmem_limit_bytes=VMEM_BYTES),
        cost_estimate=pl.CostEstimate(flops=14_000_000_000, bytes_accessed=10_000_000, transcendentals=13_000_000),
        name="attend",
    )(core, own, kv, own, other)


def gate_kernel(mod, cn, place, wg, wog, gate_out, og_out):
    samples, tokens, width = mod.shape
    rows = samples * tokens
    og_out[...] = jax.nn.sigmoid(dot(cn[...].reshape(rows, cn.shape[2]), wog[...])).reshape(og_out.shape)
    columns = GROUP * HEAD
    low = place[0:columns]
    high = place[columns:2 * columns]
    for g in range(HEADS // GROUP):
        w = wg[:, g * columns:(g + 1) * columns]
        w_low = dot(w, low).astype(BF)
        w_high = dot(w, high).astype(BF)
        for p in range(samples // 2):
            value = dot(mod[2 * p], w_low) + dot(mod[2 * p + 1], w_high)
            gate_out[p, :, g * GROUP * LANES:(g + 1) * GROUP * LANES] = jax.nn.sigmoid(value)


def gates(mod, cn, place, wg, wog):
    samples, tokens, width = mod.shape
    return pl.pallas_call(
        gate_kernel,
        out_shape=[
            jax.ShapeDtypeStruct((samples // 2, tokens, HEADS * LANES), F32),
            jax.ShapeDtypeStruct(mod.shape, F32),
        ],
        compiler_params=pltpu.CompilerParams(vmem_limit_bytes=VMEM_BYTES),
        cost_estimate=pl.CostEstimate(flops=4_000_000_000, bytes_accessed=9_000_000, transcendentals=1_000_000),
        name="gates",
    )(mod, cn, place, wg, wog)


def out_kernel(attended, gate, og, act, wo, out, low, high):
    samples, tokens, width = act.shape
    low[...] = jnp.zeros_like(low)
    high[...] = jnp.zeros_like(high)
    for h in range(HEADS):
        rows = wo[h * HEAD:(h + 1) * HEAD]
        low[h * LANES:h * LANES + HEAD] = rows
        high[h * LANES + 64:h * LANES + 64 + HEAD] = rows
    for p in range(samples // 2):
        gated = jnp.concatenate(
            [
                (attended[h, :, p * LANES:(p + 1) * LANES].astype(F32) * gate[p, :, h * LANES:(h + 1) * LANES]).astype(BF)
                for h in range(HEADS)
            ],
            axis=1,
        )
        for s, table in ((2 * p, low), (2 * p + 1, high)):
            out[s] = (act[s].astype(F32) + og[s] * dot(gated, table[...])).astype(BF)


def project_out(attended, gate, og, act, wo):
    width = act.shape[2]
    return pl.pallas_call(
        out_kernel,
        out_shape=jax.ShapeDtypeStruct(act.shape, BF),
        scratch_shapes=[pltpu.VMEM((HEADS * LANES, width), BF)] * 2,
        compiler_params=pltpu.CompilerParams(vmem_limit_bytes=VMEM_BYTES),
        cost_estimate=pl.CostEstimate(flops=2_000_000_000, bytes_accessed=6_000_000, transcendentals=0),
        name="out",
    )(attended, gate, og, act, wo)


def per_device(
    activations,
    conditioning,
    pair_features,
    key_mask,
    w_scale,
    w_shift,
    w_query,
    w_key,
    w_value,
    w_gate,
    w_out,
    w_outgate,
    w_bias,
):
    tokens = activations.shape[1]
    kv_place, q_place = placement()
    kv, q, modulated, cond_norm = project_qkv(
        activations, conditioning, key_mask.reshape(1, tokens), kv_place, q_place, w_scale, w_shift, w_query, w_key, w_value
    )
    exchange = lambda a: lax.all_to_all(a, XZ, 0, 0, tiled=True)
    bias = project_bias(pair_features, w_bias, q)
    kv, bias = lax.optimization_barrier((exchange(kv), bias))
    kv = lax.all_gather(kv, "y", axis=0)
    own = exchange(bias)
    other = lax.ppermute(own, "co", [(0, 1), (1, 0)])
    gate, out_gate = gates(modulated, cond_norm, q_place, w_gate, w_outgate)
    other, gate, out_gate = lax.optimization_barrier((other, gate, out_gate))
    core = lax.axis_index("co").astype(jnp.int32).reshape(1)
    attended = attend(
        core,
        kv.reshape(4, 2, 4, 2, tokens, kv.shape[-1]),
        own.reshape(8, 2, tokens, own.shape[-1]),
        other.reshape(8, 2, tokens, own.shape[-1]),
    )
    attended = exchange(attended.reshape(HEADS, tokens, 2 * LANES))
    return project_out(attended, gate, out_gate, activations, w_out)


def solution(mesh):
    fine = Mesh(mesh.devices.reshape(2, 4, 4, 2, 2), ("zh", "x", "y", "zl", "co"))
    wide, narrow = ("zh", "x", "y"), ("zl", "co")
    in_specs = (
        P(narrow, wide, None),
        P(narrow, wide, None),
        P(wide, narrow, None),
        P(wide),
    ) + (P(),) * 9
    return jax.shard_map(
        per_device, mesh=fine, in_specs=in_specs, out_specs=P(narrow, wide, None), check_vma=False
    )
```

```python
import math

import jax
import jax.numpy as jnp
import numpy as np
from jax import lax
from jax.experimental import pallas as pl
from jax.experimental.pallas import tpu as pltpu
from jax.sharding import Mesh, PartitionSpec as P

EPSILON = 1e-05
NEGATIVE = -1e30
LOG2E = math.log2(math.e)
HEADS = 16
HEAD = 48
LANES = 128
GROUP = 8
MARK_LANE = 95
PAD_LANE = 96
SUM_LANE = 97
XZ = ("zh", "x", "zl")
BF = jnp.bfloat16
F32 = jnp.float32
VMEM_BYTES = 56 * 1024 * 1024
NT = (((1,), (1,)), ((), ()))


def layer_norm(entries):
    entries = entries.astype(F32)
    row_mean = jnp.mean(entries, axis=-1, keepdims=True)
    centered = entries - row_mean
    variance = jnp.mean(centered * centered, axis=-1, keepdims=True)
    return centered * lax.rsqrt(variance + EPSILON)


def dot(left, right):
    return jnp.dot(left, right, preferred_element_type=F32)


def placement():
    table = np.zeros((2, 2, GROUP, HEAD, GROUP, LANES), np.float32)
    for head in range(GROUP):
        for channel in range(HEAD):
            for which, offset in ((0, HEAD), (1, 64)):
                table[which, 0, head, channel, head, channel] = 1
                table[which, 1, head, channel, head, offset + channel] = 1
    table = table.reshape(2, 2 * GROUP * HEAD, GROUP * LANES)
    return jnp.asarray(table[0], BF), jnp.asarray(table[1], BF)


def qkv_kernel(act, cond, mask, kv_place, q_place, ws, wsh, wq, wk, wv, kv_out, q_out, mod_out, cn_out, mod):
    samples, tokens, width = act.shape
    rows = samples * tokens

    @pl.when(pl.program_id(0) == 0)
    def _():
        cond_norm = layer_norm(cond[...].reshape(rows, cond.shape[2])).astype(BF)
        normed = layer_norm(act[...].reshape(rows, width))
        modulated = jax.nn.sigmoid(dot(cond_norm, ws[...])) * normed + dot(cond_norm, wsh[...])
        mod[...] = modulated.astype(BF)
        mod_out[...] = mod[...].reshape(mod_out.shape)
        cn_out[...] = cond_norm.reshape(cn_out.shape)

    modulated = mod[...]
    k = dot(modulated, wk[...]).astype(BF)
    v = dot(modulated, wv[...]).astype(BF)
    placed = dot(jnp.concatenate([k, v], axis=1), kv_place[...])
    lane = lax.broadcasted_iota(jnp.int32, (tokens, LANES), 1)
    square = (tokens, tokens)
    diagonal = lax.broadcasted_iota(jnp.int32, square, 0) == lax.broadcasted_iota(jnp.int32, square, 1)
    padded = jnp.broadcast_to(jnp.where(mask[...] > 0, 0.0, 1.0), square)
    padded = jnp.sum(jnp.where(diagonal, padded, 0.0), axis=1, keepdims=True)
    marked = (lane == MARK_LANE) & (padded > 0.5)
    for h in range(GROUP):
        tile = placed[:, h * LANES:(h + 1) * LANES]
        last = tile[3 * tokens:]
        for s in range(3):
            spare = pltpu.roll(last, 96 - 32 * s, axis=1)
            merged = jnp.where(lane < 96, tile[s * tokens:(s + 1) * tokens], spare)
            if s == 0:
                merged = jnp.where(marked, NEGATIVE, merged)
            kv_out[h, :, s * LANES:(s + 1) * LANES] = merged.astype(BF)
    q = (dot(modulated, wq[...]) * (LOG2E / math.sqrt(HEAD))).astype(BF)
    first = jnp.concatenate([q[:tokens], q[2 * tokens:3 * tokens]], axis=0)
    second = jnp.concatenate([q[tokens:2 * tokens], q[3 * tokens:]], axis=0)
    placed = dot(jnp.concatenate([first, second], axis=1), q_place[...]).astype(BF)
    for p in range(samples // 2):
        for h in range(GROUP):
            q_out[h, :, p * LANES:(p + 1) * LANES] = placed[p * tokens:(p + 1) * tokens, h * LANES:(h + 1) * LANES]


def project_qkv(act, cond, mask, kv_place, q_place, ws, wsh, wq, wk, wv):
    samples, tokens, width = act.shape
    steps = HEADS // GROUP
    columns = GROUP * HEAD
    whole = lambda a: pl.BlockSpec(a.shape, lambda g: (0,) * a.ndim)
    part = pl.BlockSpec((width, columns), lambda g: (0, g))
    return pl.pallas_call(
        qkv_kernel,
        grid=(steps,),
        in_specs=[whole(act), whole(cond), whole(mask), whole(kv_place), whole(q_place), whole(ws), whole(wsh), part, part, part],
        out_specs=[
            pl.BlockSpec((GROUP, tokens, 3 * LANES), lambda g: (g, 0, 0)),
            pl.BlockSpec((GROUP, tokens, 2 * LANES), lambda g: (g, 0, 0)),
            whole(act),
            whole(cond),
        ],
        out_shape=[
            jax.ShapeDtypeStruct((HEADS, tokens, 3 * LANES), BF),
            jax.ShapeDtypeStruct((HEADS, tokens, 2 * LANES), BF),
            jax.ShapeDtypeStruct(act.shape, BF),
            jax.ShapeDtypeStruct(cond.shape, BF),
        ],
        scratch_shapes=[pltpu.VMEM((samples * tokens, width), BF)],
        compiler_params=pltpu.CompilerParams(vmem_limit_bytes=VMEM_BYTES),
        cost_estimate=pl.CostEstimate(flops=4_000_000_000, bytes_accessed=10_000_000, transcendentals=300_000),
        name="qkv",
    )(act, cond, mask, kv_place, q_place, ws, wsh, wq, wk, wv)


def bias_kernel(pair, w_bias, q, out, rows):
    count, keys, channels = pair.shape
    wt = w_bias[...]
    zero = jnp.zeros((HEADS, channels), BF)
    part = jnp.full((HEADS, channels), 1.0 / channels, BF)
    weights = jnp.concatenate(
        [jnp.concatenate([wt, zero], axis=1), jnp.concatenate([zero, part], axis=1)], axis=0
    )
    for i in range(count):
        x = pair[i].astype(F32)
        c = (x - jnp.mean(x, axis=1, keepdims=True)).astype(BF)
        both = jnp.concatenate([c, c * c], axis=1)
        r = lax.dot_general(weights, both, NT, preferred_element_type=F32)
        rows[i] = r[:HEADS] * (lax.rsqrt(r[HEADS:] + EPSILON) * LOG2E)
    out[:, :, :keys] = jnp.swapaxes(rows[...], 0, 1).astype(BF)
    out[:, :, keys:] = q[...]


def project_bias(pair, w_bias, q):
    queries, keys, channels = pair.shape
    step = 16
    extent = keys + q.shape[2]
    return pl.pallas_call(
        bias_kernel,
        grid=(queries // step,),
        in_specs=[
            pl.BlockSpec((step, keys, channels), lambda i: (i, 0, 0)),
            pl.BlockSpec(w_bias.shape, lambda i: (0, 0)),
            pl.BlockSpec((HEADS, step, q.shape[2]), lambda i: (0, i, 0)),
        ],
        out_specs=pl.BlockSpec((HEADS, step, extent), lambda i: (0, i, 0)),
        out_shape=jax.ShapeDtypeStruct((HEADS, queries, extent), BF),
        scratch_shapes=[pltpu.VMEM((step, HEADS, keys), F32)],
        compiler_params=pltpu.CompilerParams(vmem_limit_bytes=VMEM_BYTES),
        cost_estimate=pl.CostEstimate(flops=10_000_000_000, bytes_accessed=15_000_000, transcendentals=100_000),
        name="bias",
    )(pair, w_bias, q)


T = 4


def attend_kernel(place, q, near, up, far_low, far_high, down, own, other, out, keys):
    tokens = q.shape[2]
    chunk = 8 * tokens
    core, row = place[0], place[1]
    lane_k = lax.broadcasted_iota(jnp.int32, (tokens, LANES), 1)

    @pl.when(pl.program_id(1) == 0)
    def _():
        for z in range(2):
            sources = (near.at[z], up.at[z], (far_low, far_high)[z].at[0], down.at[z])
            for o in range(2):
                quarter = core if o == 0 else 1 - core
                for low in range(2):
                    for step, source in enumerate(sources):
                        block = low * 4 + lax.rem(row + 4 - step, 4)
                        at = pl.ds(pl.multiple_of((z * 2 + o) * chunk + block * tokens, 16), tokens)
                        tiles = [source[2 * quarter + low, 0, :, i * LANES:(i + 1) * LANES] for i in range(3)]
                        wide = [t.astype(F32) for t in tiles]
                        pad = jnp.where(pltpu.roll(wide[0], PAD_LANE - MARK_LANE, axis=1) < 0.5 * NEGATIVE, NEGATIVE, 0.0)
                        tail = jnp.where(lane_k == PAD_LANE, pad, jnp.where(lane_k == SUM_LANE, 1.0, 0.0)).astype(BF)
                        for s in range(3):
                            keys[s, at] = jnp.where(lane_k < 96, tiles[s], tail)
                        last = jnp.where(
                            lane_k < 32,
                            pltpu.roll(wide[0], 32, axis=1),
                            jnp.where(lane_k < 64, pltpu.roll(wide[1], 64, axis=1), pltpu.roll(wide[2], 96, axis=1)),
                        ).astype(BF)
                        keys[3, at] = jnp.where(lane_k < 96, last, tail)

    first_sample = 2 * pl.program_id(1)
    span = T * tokens
    lane = lax.broadcasted_iota(jnp.int32, (span, LANES), 1)
    pad_one = jnp.where(lane == PAD_LANE, 1.0, 0.0).astype(BF)
    blocks = [(t, s) for t in range(8 // T) for s in range(2)]

    def scores_of(t, s, c):
        pair_q = q[t * T:(t + 1) * T, 0].reshape(span, LANES)
        if s == 1:
            pair_q = pltpu.roll(pair_q.astype(F32), 64, axis=1).astype(BF)
        mine = jnp.where(lane < HEAD, pair_q, pad_one)
        part = lax.dot_general(
            mine, keys[first_sample + s, c * chunk:(c + 1) * chunk], NT, preferred_element_type=F32
        )
        b = (own if c % 2 == 0 else other)[t * T:(t + 1) * T, c // 2].reshape(span, chunk)
        return part + b.astype(F32)

    current = [scores_of(*blocks[0], c) for c in range(4)]
    for i, (t, s) in enumerate(blocks):
        tops = [jnp.max(part, axis=1, keepdims=True) for part in current]
        top = jnp.maximum(jnp.maximum(tops[0], tops[1]), jnp.maximum(tops[2], tops[3]))
        following, total = [], None
        for c in range(4):
            if i + 1 < len(blocks):
                following.append(scores_of(*blocks[i + 1], c))
            p = jnp.exp2(current[c] - top).astype(BF)
            part = dot(p, keys[first_sample + s, c * chunk:(c + 1) * chunk])
            total = part if total is None else total + part
        current = following
        result = total / total[:, SUM_LANE:SUM_LANE + 1]
        if s == 0:
            low = pltpu.roll(result, LANES - HEAD, axis=1)
        else:
            high = pltpu.roll(result, 64 - HEAD, axis=1)
            merged = jnp.where(lane < 64, low, high).astype(BF)
            out[t * T:(t + 1) * T, 0] = merged.reshape(T, tokens, LANES)


def attend(place, kv, own, other):
    tokens = own.shape[2]
    chunk = 8 * tokens
    b_spec = pl.BlockSpec((8, 2, tokens, chunk), lambda z, p, c: (0, 0, 0, 0))
    return pl.pallas_call(
        attend_kernel,
        grid_spec=pltpu.PrefetchScalarGridSpec(
            num_scalar_prefetch=1,
            grid=(2, 2),
            in_specs=[
                pl.BlockSpec((8, 1, tokens, LANES), lambda z, p, c: (0, z, 0, chunk // LANES + p)),
            ]
            + [pl.BlockSpec((a.shape[0], 4, 1, tokens, 3 * LANES), lambda z, p, c: (0, 0, z, 0, 0)) for a in kv]
            + [
                b_spec,
                b_spec,
            ],
            out_specs=pl.BlockSpec((8, 1, tokens, LANES), lambda z, p, c: (0, z, 0, p)),
            scratch_shapes=[pltpu.VMEM((4, 4 * chunk, LANES), BF)],
        ),
        out_shape=jax.ShapeDtypeStruct((8, 2, tokens, 2 * LANES), BF),
        compiler_params=pltpu.CompilerParams(vmem_limit_bytes=VMEM_BYTES),
        cost_estimate=pl.CostEstimate(flops=14_000_000_000, bytes_accessed=10_000_000, transcendentals=13_000_000),
        name="attend",
    )(place, own, *kv, own, other)


def gate_kernel(mod, cn, place, wg, wog, gate_out, og_out):
    samples, tokens, width = mod.shape
    rows = samples * tokens
    og_out[...] = jax.nn.sigmoid(dot(cn[...].reshape(rows, cn.shape[2]), wog[...])).reshape(og_out.shape)
    columns = GROUP * HEAD
    low = place[0:columns]
    high = place[columns:2 * columns]
    for g in range(HEADS // GROUP):
        w = wg[:, g * columns:(g + 1) * columns]
        w_low = dot(w, low).astype(BF)
        w_high = dot(w, high).astype(BF)
        for p in range(samples // 2):
            value = dot(mod[2 * p], w_low) + dot(mod[2 * p + 1], w_high)
            gate_out[p, :, g * GROUP * LANES:(g + 1) * GROUP * LANES] = jax.nn.sigmoid(value)


def gates(mod, cn, place, wg, wog):
    samples, tokens, width = mod.shape
    return pl.pallas_call(
        gate_kernel,
        out_shape=[
            jax.ShapeDtypeStruct((samples // 2, tokens, HEADS * LANES), F32),
            jax.ShapeDtypeStruct(mod.shape, F32),
        ],
        compiler_params=pltpu.CompilerParams(vmem_limit_bytes=VMEM_BYTES),
        cost_estimate=pl.CostEstimate(flops=4_000_000_000, bytes_accessed=9_000_000, transcendentals=1_000_000),
        name="gates",
    )(mod, cn, place, wg, wog)


def out_kernel(attended, gate, og, act, wo, out, low, high):
    samples, tokens, width = act.shape
    low[...] = jnp.zeros_like(low)
    high[...] = jnp.zeros_like(high)
    for h in range(HEADS):
        rows = wo[h * HEAD:(h + 1) * HEAD]
        low[h * LANES:h * LANES + HEAD] = rows
        high[h * LANES + 64:h * LANES + 64 + HEAD] = rows
    for p in range(samples // 2):
        gated = jnp.concatenate(
            [
                (attended[h, :, p * LANES:(p + 1) * LANES].astype(F32) * gate[p, :, h * LANES:(h + 1) * LANES]).astype(BF)
                for h in range(HEADS)
            ],
            axis=1,
        )
        for s, table in ((2 * p, low), (2 * p + 1, high)):
            out[s] = (act[s].astype(F32) + og[s] * dot(gated, table[...])).astype(BF)


def project_out(attended, gate, og, act, wo):
    width = act.shape[2]
    return pl.pallas_call(
        out_kernel,
        out_shape=jax.ShapeDtypeStruct(act.shape, BF),
        scratch_shapes=[pltpu.VMEM((HEADS * LANES, width), BF)] * 2,
        compiler_params=pltpu.CompilerParams(vmem_limit_bytes=VMEM_BYTES),
        cost_estimate=pl.CostEstimate(flops=2_000_000_000, bytes_accessed=6_000_000, transcendentals=0),
        name="out",
    )(attended, gate, og, act, wo)


def ring(block, step):
    return lax.ppermute(block, "y", [(i, (i + step) % 4) for i in range(4)])


def per_device(
    activations,
    conditioning,
    pair_features,
    key_mask,
    w_scale,
    w_shift,
    w_query,
    w_key,
    w_value,
    w_gate,
    w_out,
    w_outgate,
    w_bias,
):
    tokens = activations.shape[1]
    kv_place, q_place = placement()
    kv, q, modulated, cond_norm = project_qkv(
        activations, conditioning, key_mask.reshape(1, tokens), kv_place, q_place, w_scale, w_shift, w_query, w_key, w_value
    )
    exchange = lambda a: lax.all_to_all(a, XZ, 0, 0, tiled=True)
    bias = project_bias(pair_features, w_bias.T, q)
    kv, bias = lax.optimization_barrier((exchange(kv), bias))
    up, down = ring(kv, 1), ring(kv, 3)
    far = (ring(up[:HEADS // 2], 1), ring(down[HEADS // 2:], 3))
    own = exchange(bias)
    gate, out_gate = gates(modulated, cond_norm, q_place, w_gate, w_outgate)
    own, up, down, far, gate, out_gate = lax.optimization_barrier((own, up, down, far, gate, out_gate))
    other = lax.ppermute(own, "co", [(0, 1), (1, 0)])
    place = jnp.stack([lax.axis_index("co"), lax.axis_index("y")]).astype(jnp.int32)
    attended = attend(
        place,
        [a.reshape(-1, 4, 2, tokens, kv.shape[-1]) for a in (kv, up, *far, down)],
        own.reshape(8, 2, tokens, own.shape[-1]),
        other.reshape(8, 2, tokens, own.shape[-1]),
    )
    attended = exchange(attended.reshape(HEADS, tokens, 2 * LANES))
    return project_out(attended, gate, out_gate, activations, w_out)


def solution(mesh):
    fine = Mesh(mesh.devices.reshape(2, 4, 4, 2, 2), ("zh", "x", "y", "zl", "co"))
    wide, narrow = ("zh", "x", "y"), ("zl", "co")
    in_specs = (
        P(narrow, wide, None),
        P(narrow, wide, None),
        P(wide, narrow, None),
        P(wide),
    ) + (P(),) * 9
    return jax.shard_map(
        per_device, mesh=fine, in_specs=in_specs, out_specs=P(narrow, wide, None), check_vma=False
    )
```

```python
import math

import jax
import jax.numpy as jnp
import numpy as np
from jax import lax
from jax.experimental import pallas as pl
from jax.experimental.pallas import tpu as pltpu
from jax.sharding import Mesh, PartitionSpec as P

EPSILON = 1e-05
NEGATIVE = -1e30
LOG2E = math.log2(math.e)
HEADS = 16
HEAD = 48
LANES = 128
GROUP = 8
MARK_LANE = 95
PAD_LANE = 96
SUM_LANE = 97
XZ = ("zh", "x", "zl")
BF = jnp.bfloat16
F32 = jnp.float32
VMEM_BYTES = 56 * 1024 * 1024
NT = (((1,), (1,)), ((), ()))


def layer_norm(entries):
    entries = entries.astype(F32)
    row_mean = jnp.mean(entries, axis=-1, keepdims=True)
    centered = entries - row_mean
    variance = jnp.mean(centered * centered, axis=-1, keepdims=True)
    return centered * lax.rsqrt(variance + EPSILON)


def dot(left, right):
    return jnp.dot(left, right, preferred_element_type=F32)


def placement():
    table = np.zeros((2, 2, GROUP, HEAD, GROUP, LANES), np.float32)
    for head in range(GROUP):
        for channel in range(HEAD):
            for which, offset in ((0, HEAD), (1, 64)):
                table[which, 0, head, channel, head, channel] = 1
                table[which, 1, head, channel, head, offset + channel] = 1
    table = table.reshape(2, 2 * GROUP * HEAD, GROUP * LANES)
    pairs = np.zeros((HEADS // 2, 2 * HEAD, HEADS // 2, LANES), np.float32)
    for pair in range(HEADS // 2):
        for channel in range(2 * HEAD):
            pairs[pair, channel, pair, channel] = 1
    pairs = pairs.reshape(HEADS * HEAD, HEADS // 2 * LANES)
    return jnp.asarray(table[0], BF), jnp.asarray(table[1], BF), jnp.asarray(pairs, BF)


def qkv_kernel(act, cond, mask, kv_place, q_place, ws, wsh, wq, wk, wv, kv_out, q_out, mod_out, cn_out, mod):
    samples, tokens, width = act.shape
    rows = samples * tokens

    @pl.when(pl.program_id(0) == 0)
    def _():
        cond_norm = layer_norm(cond[...].reshape(rows, cond.shape[2])).astype(BF)
        normed = layer_norm(act[...].reshape(rows, width))
        modulated = jax.nn.sigmoid(dot(cond_norm, ws[...])) * normed + dot(cond_norm, wsh[...])
        mod[...] = modulated.astype(BF)
        mod_out[...] = mod[...].reshape(mod_out.shape)
        cn_out[...] = cond_norm.reshape(cn_out.shape)

    modulated = mod[...]
    k = dot(modulated, wk[...]).astype(BF)
    v = dot(modulated, wv[...]).astype(BF)
    placed = dot(jnp.concatenate([k, v], axis=1), kv_place[...])
    lane = lax.broadcasted_iota(jnp.int32, (tokens, LANES), 1)
    square = (tokens, tokens)
    diagonal = lax.broadcasted_iota(jnp.int32, square, 0) == lax.broadcasted_iota(jnp.int32, square, 1)
    padded = jnp.broadcast_to(jnp.where(mask[...] > 0, 0.0, 1.0), square)
    padded = jnp.sum(jnp.where(diagonal, padded, 0.0), axis=1, keepdims=True)
    marked = (lane == MARK_LANE) & (padded > 0.5)
    for h in range(GROUP):
        tile = placed[:, h * LANES:(h + 1) * LANES]
        last = tile[3 * tokens:]
        for s in range(3):
            spare = pltpu.roll(last, 96 - 32 * s, axis=1)
            merged = jnp.where(lane < 96, tile[s * tokens:(s + 1) * tokens], spare)
            if s == 0:
                merged = jnp.where(marked, NEGATIVE, merged)
            kv_out[h, :, s * LANES:(s + 1) * LANES] = merged.astype(BF)
    q = (dot(modulated, wq[...]) * (LOG2E / math.sqrt(HEAD))).astype(BF)
    first = jnp.concatenate([q[:tokens], q[2 * tokens:3 * tokens]], axis=0)
    second = jnp.concatenate([q[tokens:2 * tokens], q[3 * tokens:]], axis=0)
    placed = dot(jnp.concatenate([first, second], axis=1), q_place[...]).astype(BF)
    for p in range(samples // 2):
        for h in range(GROUP):
            q_out[h, :, p * LANES:(p + 1) * LANES] = placed[p * tokens:(p + 1) * tokens, h * LANES:(h + 1) * LANES]


def project_qkv(act, cond, mask, kv_place, q_place, ws, wsh, wq, wk, wv):
    samples, tokens, width = act.shape
    steps = HEADS // GROUP
    columns = GROUP * HEAD
    whole = lambda a: pl.BlockSpec(a.shape, lambda g: (0,) * a.ndim)
    part = pl.BlockSpec((width, columns), lambda g: (0, g))
    return pl.pallas_call(
        qkv_kernel,
        grid=(steps,),
        in_specs=[whole(act), whole(cond), whole(mask), whole(kv_place), whole(q_place), whole(ws), whole(wsh), part, part, part],
        out_specs=[
            pl.BlockSpec((GROUP, tokens, 3 * LANES), lambda g: (g, 0, 0)),
            pl.BlockSpec((GROUP, tokens, 2 * LANES), lambda g: (g, 0, 0)),
            whole(act),
            whole(cond),
        ],
        out_shape=[
            jax.ShapeDtypeStruct((HEADS, tokens, 3 * LANES), BF),
            jax.ShapeDtypeStruct((HEADS, tokens, 2 * LANES), BF),
            jax.ShapeDtypeStruct(act.shape, BF),
            jax.ShapeDtypeStruct(cond.shape, BF),
        ],
        scratch_shapes=[pltpu.VMEM((samples * tokens, width), BF)],
        compiler_params=pltpu.CompilerParams(vmem_limit_bytes=VMEM_BYTES),
        cost_estimate=pl.CostEstimate(flops=4_000_000_000, bytes_accessed=10_000_000, transcendentals=300_000),
        name="qkv",
    )(act, cond, mask, kv_place, q_place, ws, wsh, wq, wk, wv)


def bias_kernel(pair, w_bias, q, out, rows):
    count, keys, channels = pair.shape
    wt = w_bias[...]
    zero = jnp.zeros((HEADS, channels), BF)
    part = jnp.full((HEADS, channels), 1.0 / channels, BF)
    weights = jnp.concatenate(
        [jnp.concatenate([wt, zero], axis=1), jnp.concatenate([zero, part], axis=1)], axis=0
    )
    for i in range(count):
        x = pair[i].astype(F32)
        c = (x - jnp.mean(x, axis=1, keepdims=True)).astype(BF)
        both = jnp.concatenate([c, c * c], axis=1)
        r = lax.dot_general(weights, both, NT, preferred_element_type=F32)
        rows[i] = r[:HEADS] * (lax.rsqrt(r[HEADS:] + EPSILON) * LOG2E)
    out[:, :, :keys] = jnp.swapaxes(rows[...], 0, 1).astype(BF)
    out[:, :, keys:] = q[...]


def project_bias(pair, w_bias, q):
    queries, keys, channels = pair.shape
    step = 16
    extent = keys + q.shape[2]
    return pl.pallas_call(
        bias_kernel,
        grid=(queries // step,),
        in_specs=[
            pl.BlockSpec((step, keys, channels), lambda i: (i, 0, 0)),
            pl.BlockSpec(w_bias.shape, lambda i: (0, 0)),
            pl.BlockSpec((HEADS, step, q.shape[2]), lambda i: (0, i, 0)),
        ],
        out_specs=pl.BlockSpec((HEADS, step, extent), lambda i: (0, i, 0)),
        out_shape=jax.ShapeDtypeStruct((HEADS, queries, extent), BF),
        scratch_shapes=[pltpu.VMEM((step, HEADS, keys), F32)],
        compiler_params=pltpu.CompilerParams(vmem_limit_bytes=VMEM_BYTES),
        cost_estimate=pl.CostEstimate(flops=10_000_000_000, bytes_accessed=15_000_000, transcendentals=100_000),
        name="bias",
    )(pair, w_bias, q)


T = 4
PIECE = 128
LIMIT = 2.0**100


def lay_kernel(place, near, up, far_low, far_high, down, keys):
    tokens = near.shape[-2]
    core, row = place[0], place[1]
    lane = lax.broadcasted_iota(jnp.int32, (tokens, LANES), 1)
    for z in range(2):
        parts = (near.at[z], up.at[z], (far_low, far_high)[z].at[0], down.at[z])
        for o in range(2):
            quarter = core if o == 0 else 1 - core
            for low in range(2):
                for step, part in enumerate(parts):
                    block = (z * 2 + o) * 8 + low * 4 + lax.rem(row + 4 - step, 4)
                    at = pl.ds(pl.multiple_of(block * tokens, 16), tokens)
                    tiles = [part[2 * quarter + low, 0, :, i * LANES:(i + 1) * LANES] for i in range(3)]
                    wide = [t.astype(F32) for t in tiles]
                    mark = pltpu.roll(wide[0], PAD_LANE - MARK_LANE, axis=1)
                    pad = jnp.where(mark < 0.5 * NEGATIVE, NEGATIVE, 0.0)
                    tail = jnp.where(lane == PAD_LANE, pad, jnp.where(lane == SUM_LANE, 1.0, 0.0)).astype(BF)
                    for s in range(3):
                        keys[0, s, at] = jnp.where(lane < 96, tiles[s], tail)
                    last = jnp.where(
                        lane < 32,
                        pltpu.roll(wide[0], 32, axis=1),
                        jnp.where(lane < 64, pltpu.roll(wide[1], 64, axis=1), pltpu.roll(wide[2], 96, axis=1)),
                    ).astype(BF)
                    keys[0, 3, at] = jnp.where(lane < 96, last, tail)


def lay_keys(place, kv):
    tokens = kv[0].shape[3]
    extent = 32 * tokens
    return pl.pallas_call(
        lay_kernel,
        grid_spec=pltpu.PrefetchScalarGridSpec(
            num_scalar_prefetch=1,
            grid=(2,),
            in_specs=[pl.BlockSpec((a.shape[0], 4, 1, tokens, 3 * LANES), lambda z, c: (0, 0, z, 0, 0)) for a in kv],
            out_specs=pl.BlockSpec((1, 4, extent, LANES), lambda z, c: (z, 0, 0, 0)),
        ),
        out_shape=jax.ShapeDtypeStruct((2, 4, extent, LANES), BF),
        compiler_params=pltpu.CompilerParams(vmem_limit_bytes=VMEM_BYTES),
        cost_estimate=pl.CostEstimate(flops=40_000_000_000, bytes_accessed=10_000_000, transcendentals=0),
        name="lay",
    )(place, *kv)


def attend_kernel(q, keys, own, other, out):
    tokens = q.shape[2]
    chunk = 8 * tokens
    span = T * tokens
    lane = lax.broadcasted_iota(jnp.int32, (span, LANES), 1)
    pad_one = jnp.where(lane == PAD_LANE, 1.0, 0.0).astype(BF)

    def query(t, s):
        pair_q = q[pl.ds(t * T, T), 0].reshape(span, LANES)
        if s == 1:
            pair_q = pltpu.roll(pair_q.astype(F32), 64, axis=1).astype(BF)
        return jnp.where(lane < HEAD, pair_q, pad_one)

    def scores(t, s, at, width):
        part = lax.dot_general(query(t, s), keys[0, s, at:at + width], NT, preferred_element_type=F32)
        columns = at % chunk
        bias = own if at // chunk % 2 == 0 else other
        bias = bias[pl.ds(t * T, T), at // chunk // 2, :, columns:columns + width].reshape(span, width)
        return part + bias.astype(F32)

    def values(p, s, at, width):
        return dot(p, keys[0, s, at:at + width])

    def store(t, pair):
        low = pltpu.roll(pair[0], LANES - HEAD, axis=1)
        high = pltpu.roll(pair[1], 64 - HEAD, axis=1)
        merged = jnp.where(lane < 64, low, high).astype(BF)
        out[pl.ds(t * T, T), 0] = merged.reshape(T, tokens, LANES)

    pieces = [(t, s, at) for t in range(8 // T) for s in range(2) for at in range(0, 4 * chunk, PIECE)]
    following = scores(*pieces[0], PIECE)
    top, total, pair, worst = None, None, [], jnp.float32(0.0)
    for i, (t, s, at) in enumerate(pieces):
        current = following
        if at == 0:
            top, total = jnp.max(current, axis=1, keepdims=True), None
        if i + 1 < len(pieces):
            following = scores(*pieces[i + 1], PIECE)
        part = values(jnp.exp2(current - top).astype(BF), s, at, PIECE)
        total = part if total is None else total + part
        if at == 4 * chunk - PIECE:
            weight = total[:, SUM_LANE:SUM_LANE + 1]
            worst = jnp.maximum(worst, jnp.max(weight))
            pair.append(total / weight)
            if s == 1:
                store(t, pair)
                pair = []

    @pl.when(jnp.logical_not(worst < LIMIT))
    def _():
        def block(t, carried):
            pair = []
            for s in range(2):
                top = total = None
                for at in range(0, 4 * chunk, chunk):
                    peak = jnp.max(scores(t, s, at, chunk), axis=1, keepdims=True)
                    top = peak if top is None else jnp.maximum(top, peak)
                for at in range(0, 4 * chunk, chunk):
                    p = jnp.exp2(scores(t, s, at, chunk) - top).astype(BF)
                    part = values(p, s, at, chunk)
                    total = part if total is None else total + part
                pair.append(total / total[:, SUM_LANE:SUM_LANE + 1])
            store(t, pair)
            return carried

        lax.fori_loop(0, 8 // T, block, 0)


def attend(keys, own, other):
    tokens = own.shape[2]
    chunk = 8 * tokens
    b_spec = pl.BlockSpec((8, 2, tokens, chunk), lambda z, p: (0, 0, 0, 0))
    return pl.pallas_call(
        attend_kernel,
        grid=(2, 2),
        in_specs=[
            pl.BlockSpec((8, 1, tokens, LANES), lambda z, p: (0, z, 0, chunk // LANES + p)),
            pl.BlockSpec((1, 2, 4 * chunk, LANES), lambda z, p: (z, p, 0, 0)),
            b_spec,
            b_spec,
        ],
        out_specs=pl.BlockSpec((8, 1, tokens, LANES), lambda z, p: (0, z, 0, p)),
        out_shape=jax.ShapeDtypeStruct((8, 2, tokens, 2 * LANES), BF),
        compiler_params=pltpu.CompilerParams(vmem_limit_bytes=VMEM_BYTES),
        cost_estimate=pl.CostEstimate(flops=14_000_000_000, bytes_accessed=10_000_000, transcendentals=13_000_000),
        name="attend",
    )(own, keys, own, other)


def gate_kernel(mod, cn, place, wg, wog, gate_out, og_out):
    samples, tokens, width = mod.shape
    rows = samples * tokens
    og_out[...] = jax.nn.sigmoid(dot(cn[...].reshape(rows, cn.shape[2]), wog[...])).reshape(og_out.shape)
    placed = dot(wg[...], place[...]).astype(BF)
    gate = jax.nn.sigmoid(dot(mod[...].reshape(rows, width), placed))
    gate_out[...] = gate.reshape(gate_out.shape)


def gates(mod, cn, place, wg, wog):
    samples, tokens, width = mod.shape
    return pl.pallas_call(
        gate_kernel,
        out_shape=[
            jax.ShapeDtypeStruct((samples, tokens, HEADS // 2 * LANES), F32),
            jax.ShapeDtypeStruct(mod.shape, F32),
        ],
        compiler_params=pltpu.CompilerParams(vmem_limit_bytes=VMEM_BYTES),
        cost_estimate=pl.CostEstimate(flops=32_000_000_000, bytes_accessed=9_000_000, transcendentals=1_000_000),
        name="gates",
    )(mod, cn, place, wg, wog)


def out_kernel(attended, gate, og, act, wo, out, table):
    samples, tokens, width = act.shape
    table[...] = jnp.zeros_like(table)
    for j in range(HEADS // 2):
        table[j * LANES:j * LANES + 96] = wo[j * 96:(j + 1) * 96]
    lane = lax.broadcasted_iota(jnp.int32, (tokens, LANES), 1)
    rows = []
    for s in range(samples):
        lanes = slice(s // 2 * LANES, (s // 2 + 1) * LANES)
        tiles = []
        for j in range(HEADS // 2):
            first = attended[2 * j, :, lanes].astype(F32)
            second = attended[2 * j + 1, :, lanes].astype(F32)
            if s % 2 == 0:
                second = pltpu.roll(second, HEAD, axis=1)
            else:
                first = pltpu.roll(first, 64, axis=1)
                second = pltpu.roll(second, 64 + HEAD, axis=1)
            both = jnp.where(lane < HEAD, first, second)
            tiles.append((both * gate[s, :, j * LANES:(j + 1) * LANES]).astype(BF))
        rows.append(jnp.concatenate(tiles, axis=1))
    projected = dot(jnp.concatenate(rows, axis=0), table[...])
    out[...] = (act[...].astype(F32) + og[...] * projected.reshape(act.shape)).astype(BF)


def project_out(attended, gate, og, act, wo):
    width = act.shape[2]
    return pl.pallas_call(
        out_kernel,
        out_shape=jax.ShapeDtypeStruct(act.shape, BF),
        scratch_shapes=[pltpu.VMEM((HEADS // 2 * LANES, width), BF)],
        compiler_params=pltpu.CompilerParams(vmem_limit_bytes=VMEM_BYTES),
        cost_estimate=pl.CostEstimate(flops=2_000_000_000, bytes_accessed=6_000_000, transcendentals=0),
        name="out",
    )(attended, gate, og, act, wo)


def ring(block, step):
    return lax.ppermute(block, "y", [(i, (i + step) % 4) for i in range(4)])


def per_device(
    activations,
    conditioning,
    pair_features,
    key_mask,
    w_scale,
    w_shift,
    w_query,
    w_key,
    w_value,
    w_gate,
    w_out,
    w_outgate,
    w_bias,
):
    tokens = activations.shape[1]
    kv_place, q_place, gate_place = placement()
    kv, q, modulated, cond_norm = project_qkv(
        activations, conditioning, key_mask.reshape(1, tokens), kv_place, q_place, w_scale, w_shift, w_query, w_key, w_value
    )
    exchange = lambda a: lax.all_to_all(a, XZ, 0, 0, tiled=True)
    bias = project_bias(pair_features, w_bias.T, q)
    kv, bias = lax.optimization_barrier((exchange(kv), bias))
    up, down = ring(kv, 1), ring(kv, 3)
    own = exchange(bias)
    gate, out_gate = gates(modulated, cond_norm, gate_place, w_gate, w_outgate)
    up, down, gate, out_gate = lax.optimization_barrier((up, down, gate, out_gate))
    far = (ring(up[:HEADS // 2], 1), ring(down[HEADS // 2:], 3))
    other = lax.ppermute(own, "co", [(0, 1), (1, 0)])
    place = jnp.stack([lax.axis_index("co"), lax.axis_index("y")]).astype(jnp.int32)
    kv = [a.reshape(-1, 4, 2, tokens, kv.shape[-1]) for a in (kv, up, *far, down)]
    own, other = (a.reshape(8, 2, tokens, own.shape[-1]) for a in (own, other))
    attended = attend(lay_keys(place, kv), own, other)
    attended = exchange(attended.reshape(HEADS, tokens, 2 * LANES))
    return project_out(attended, gate, out_gate, activations, w_out)


def solution(mesh):
    fine = Mesh(mesh.devices.reshape(2, 4, 4, 2, 2), ("zh", "x", "y", "zl", "co"))
    wide, narrow = ("zh", "x", "y"), ("zl", "co")
    in_specs = (
        P(narrow, wide, None),
        P(narrow, wide, None),
        P(wide, narrow, None),
        P(wide),
    ) + (P(),) * 9
    return jax.shard_map(
        per_device, mesh=fine, in_specs=in_specs, out_specs=P(narrow, wide, None), check_vma=False
    )
```

```python
import math

import jax
import jax.numpy as jnp
import numpy as np
from jax import lax
from jax.experimental import pallas as pl
from jax.experimental.pallas import tpu as pltpu
from jax.sharding import Mesh, PartitionSpec as P

EPSILON = 1e-05
NEGATIVE = -1e30
LOG2E = math.log2(math.e)
HEADS = 16
HEAD = 48
LANES = 128
GROUP = 8
MARK_LANE = 95
PAD_LANE = 96
SUM_LANE = 97
XZ = ("zh", "x", "zl")
BF = jnp.bfloat16
F32 = jnp.float32
VMEM_BYTES = 56 * 1024 * 1024
SMALL_VMEM_BYTES = 40 * 1024 * 1024
NT = (((1,), (1,)), ((), ()))


def layer_norm(entries):
    entries = entries.astype(F32)
    row_mean = jnp.mean(entries, axis=-1, keepdims=True)
    centered = entries - row_mean
    variance = jnp.mean(centered * centered, axis=-1, keepdims=True)
    return centered * lax.rsqrt(variance + EPSILON)


def dot(left, right):
    return jnp.dot(left, right, preferred_element_type=F32)


def placement():
    pairs = np.zeros((HEADS // 2, 2 * HEAD, HEADS // 2, LANES), np.float32)
    for pair in range(HEADS // 2):
        for channel in range(2 * HEAD):
            pairs[pair, channel, pair, channel] = 1
    return jnp.asarray(pairs.reshape(HEADS * HEAD, HEADS // 2 * LANES), BF)


def moved(columns, rows, head, to, lane):
    tile, offset = divmod(head * HEAD, LANES)
    shift = (to - offset) % LANES
    take = lambda i: columns[rows, i * LANES:(i + 1) * LANES]
    turn = lambda x: pltpu.roll(x, shift, axis=1) if shift else x
    first = turn(take(tile))
    if offset + HEAD <= LANES:
        return first
    return jnp.where(lane < to + LANES - offset, first, turn(take(tile + 1)))


def qkv_kernel(act, cond, mask, ws, wsh, wq, wk, wv, kv_out, q_out, mod_out, cn_out, mod):
    samples, tokens, width = act.shape
    rows = samples * tokens

    @pl.when(pl.program_id(0) == 0)
    def _():
        cond_norm = layer_norm(cond[...].reshape(rows, cond.shape[2])).astype(BF)
        normed = layer_norm(act[...].reshape(rows, width))
        modulated = jax.nn.sigmoid(dot(cond_norm, ws[...])) * normed + dot(cond_norm, wsh[...])
        mod[...] = modulated.astype(BF)
        mod_out[...] = mod[...].reshape(mod_out.shape)
        cn_out[...] = cond_norm.reshape(cn_out.shape)

    modulated = mod[...]
    lane = lax.broadcasted_iota(jnp.int32, (tokens, LANES), 1)
    square = (tokens, tokens)
    diagonal = lax.broadcasted_iota(jnp.int32, square, 0) == lax.broadcasted_iota(jnp.int32, square, 1)
    padded = jnp.broadcast_to(jnp.where(mask[...] > 0, 0.0, 1.0), square)
    padded = jnp.sum(jnp.where(diagonal, padded, 0.0), axis=1, keepdims=True)
    marked = (lane == MARK_LANE) & (padded > 0.5)
    sample = [slice(s * tokens, (s + 1) * tokens) for s in range(samples)]
    k = dot(modulated, wk[...])
    v = dot(modulated, wv[...])
    for h in range(GROUP):
        tile = [
            jnp.where(lane < HEAD, moved(k, row, h, 0, lane), moved(v, row, h, HEAD, lane)) for row in sample
        ]
        for s in range(3):
            spare = pltpu.roll(tile[3], 96 - 32 * s, axis=1)
            merged = jnp.where(lane < 96, tile[s], spare)
            if s == 0:
                merged = jnp.where(marked, NEGATIVE, merged)
            kv_out[h, :, s * LANES:(s + 1) * LANES] = merged.astype(BF)
    q = dot(modulated, wq[...]) * (LOG2E / math.sqrt(HEAD))
    for h in range(GROUP):
        for p in range(samples // 2):
            first = moved(q, sample[2 * p], h, 0, lane)
            second = moved(q, sample[2 * p + 1], h, 64, lane)
            q_out[h, :, p * LANES:(p + 1) * LANES] = jnp.where(lane < 64, first, second).astype(BF)


def project_qkv(act, cond, mask, ws, wsh, wq, wk, wv):
    samples, tokens, width = act.shape
    steps = HEADS // GROUP
    columns = GROUP * HEAD
    whole = lambda a: pl.BlockSpec(a.shape, lambda g: (0,) * a.ndim)
    part = pl.BlockSpec((width, columns), lambda g: (0, g))
    return pl.pallas_call(
        qkv_kernel,
        grid=(steps,),
        in_specs=[whole(act), whole(cond), whole(mask), whole(ws), whole(wsh), part, part, part],
        out_specs=[
            pl.BlockSpec((GROUP, tokens, 3 * LANES), lambda g: (g, 0, 0)),
            pl.BlockSpec((GROUP, tokens, 2 * LANES), lambda g: (g, 0, 0)),
            whole(act),
            whole(cond),
        ],
        out_shape=[
            jax.ShapeDtypeStruct((HEADS, tokens, 3 * LANES), BF),
            jax.ShapeDtypeStruct((HEADS, tokens, 2 * LANES), BF),
            jax.ShapeDtypeStruct(act.shape, BF),
            jax.ShapeDtypeStruct(cond.shape, BF),
        ],
        scratch_shapes=[pltpu.VMEM((samples * tokens, width), BF)],
        compiler_params=pltpu.CompilerParams(vmem_limit_bytes=VMEM_BYTES),
        cost_estimate=pl.CostEstimate(flops=4_000_000_000, bytes_accessed=10_000_000, transcendentals=300_000),
        name="qkv",
    )(act, cond, mask, ws, wsh, wq, wk, wv)


def bias_kernel(pair, w_bias, q, out, rows):
    count, keys, channels = pair.shape
    wt = w_bias[...]
    zero = jnp.zeros((HEADS, channels), BF)
    part = jnp.full((HEADS, channels), 1.0 / channels, BF)
    weights = jnp.concatenate(
        [jnp.concatenate([wt, zero], axis=1), jnp.concatenate([zero, part], axis=1)], axis=0
    )
    for i in range(count):
        x = pair[i].astype(F32)
        c = (x - jnp.mean(x, axis=1, keepdims=True)).astype(BF)
        both = jnp.concatenate([c, c * c], axis=1)
        r = lax.dot_general(weights, both, NT, preferred_element_type=F32)
        rows[i] = r[:HEADS] * (lax.rsqrt(r[HEADS:] + EPSILON) * LOG2E)
    out[:, :, :keys] = jnp.swapaxes(rows[...], 0, 1).astype(BF)
    out[:, :, keys:] = q[...]


def project_bias(pair, w_bias, q):
    queries, keys, channels = pair.shape
    step = 16
    extent = keys + q.shape[2]
    return pl.pallas_call(
        bias_kernel,
        grid=(queries // step,),
        in_specs=[
            pl.BlockSpec((step, keys, channels), lambda i: (i, 0, 0)),
            pl.BlockSpec(w_bias.shape, lambda i: (0, 0)),
            pl.BlockSpec((HEADS, step, q.shape[2]), lambda i: (0, i, 0)),
        ],
        out_specs=pl.BlockSpec((HEADS, step, extent), lambda i: (0, i, 0)),
        out_shape=jax.ShapeDtypeStruct((HEADS, queries, extent), BF),
        scratch_shapes=[pltpu.VMEM((step, HEADS, keys), F32)],
        compiler_params=pltpu.CompilerParams(vmem_limit_bytes=VMEM_BYTES),
        cost_estimate=pl.CostEstimate(flops=10_000_000_000, bytes_accessed=15_000_000, transcendentals=100_000),
        name="bias",
    )(pair, w_bias, q)


T = 4
PIECE = 128
LIMIT = 2.0**100


def lay_kernel(place, near, up, far_low, far_high, down, keys):
    tokens = near.shape[-2]
    core, row = place[0], place[1]
    lane = lax.broadcasted_iota(jnp.int32, (tokens, LANES), 1)
    for z in range(2):
        parts = (near.at[z], up.at[z], (far_low, far_high)[z].at[0], down.at[z])
        for o in range(2):
            quarter = core if o == 0 else 1 - core
            for low in range(2):
                for step, part in enumerate(parts):
                    block = (z * 2 + o) * 8 + low * 4 + lax.rem(row + 4 - step, 4)
                    at = pl.ds(pl.multiple_of(block * tokens, 16), tokens)
                    tiles = [part[2 * quarter + low, 0, :, i * LANES:(i + 1) * LANES] for i in range(3)]
                    wide = [t.astype(F32) for t in tiles]
                    mark = pltpu.roll(wide[0], PAD_LANE - MARK_LANE, axis=1)
                    pad = jnp.where(mark < 0.5 * NEGATIVE, NEGATIVE, 0.0)
                    tail = jnp.where(lane == PAD_LANE, pad, jnp.where(lane == SUM_LANE, 1.0, 0.0)).astype(BF)
                    for s in range(3):
                        keys[0, s, at] = jnp.where(lane < 96, tiles[s], tail)
                    last = jnp.where(
                        lane < 32,
                        pltpu.roll(wide[0], 32, axis=1),
                        jnp.where(lane < 64, pltpu.roll(wide[1], 64, axis=1), pltpu.roll(wide[2], 96, axis=1)),
                    ).astype(BF)
                    keys[0, 3, at] = jnp.where(lane < 96, last, tail)


def lay_keys(place, kv):
    tokens = kv[0].shape[3]
    extent = 32 * tokens
    return pl.pallas_call(
        lay_kernel,
        grid_spec=pltpu.PrefetchScalarGridSpec(
            num_scalar_prefetch=1,
            grid=(2,),
            in_specs=[pl.BlockSpec((a.shape[0], 4, 1, tokens, 3 * LANES), lambda z, c: (0, 0, z, 0, 0)) for a in kv],
            out_specs=pl.BlockSpec((1, 4, extent, LANES), lambda z, c: (z, 0, 0, 0)),
        ),
        out_shape=jax.ShapeDtypeStruct((2, 4, extent, LANES), BF),
        compiler_params=pltpu.CompilerParams(vmem_limit_bytes=SMALL_VMEM_BYTES),
        cost_estimate=pl.CostEstimate(flops=40_000_000_000, bytes_accessed=10_000_000, transcendentals=0),
        name="lay",
    )(place, *kv)


def attend_kernel(q, keys, own, other, out):
    tokens = q.shape[2]
    chunk = 8 * tokens
    span = T * tokens
    lane = lax.broadcasted_iota(jnp.int32, (span, LANES), 1)
    pad_one = jnp.where(lane == PAD_LANE, 1.0, 0.0).astype(BF)

    def query(t, s):
        pair_q = q[pl.ds(t * T, T), 0].reshape(span, LANES)
        if s == 1:
            pair_q = pltpu.roll(pair_q.astype(F32), 64, axis=1).astype(BF)
        return jnp.where(lane < HEAD, pair_q, pad_one)

    def scores(t, s, at, width):
        part = lax.dot_general(query(t, s), keys[0, s, at:at + width], NT, preferred_element_type=F32)
        columns = at % chunk
        bias = own if at // chunk % 2 == 0 else other
        bias = bias[pl.ds(t * T, T), at // chunk // 2, :, columns:columns + width].reshape(span, width)
        return part + bias.astype(F32)

    def values(p, s, at, width):
        return dot(p, keys[0, s, at:at + width])

    def store(t, pair):
        low = pltpu.roll(pair[0], LANES - HEAD, axis=1)
        high = pltpu.roll(pair[1], 64 - HEAD, axis=1)
        merged = jnp.where(lane < 64, low, high).astype(BF)
        out[pl.ds(t * T, T), 0] = merged.reshape(T, tokens, LANES)

    pieces = [(t, s, at) for t in range(8 // T) for s in range(2) for at in range(0, 4 * chunk, PIECE)]
    following = scores(*pieces[0], PIECE)
    top, total, pair, worst = None, None, [], jnp.float32(0.0)
    for i, (t, s, at) in enumerate(pieces):
        current = following
        if at == 0:
            top, total = jnp.max(current, axis=1, keepdims=True), None
        if i + 1 < len(pieces):
            following = scores(*pieces[i + 1], PIECE)
        part = values(jnp.exp2(current - top).astype(BF), s, at, PIECE)
        total = part if total is None else total + part
        if at == 4 * chunk - PIECE:
            weight = total[:, SUM_LANE:SUM_LANE + 1]
            worst = jnp.maximum(worst, jnp.max(weight))
            pair.append(total / weight)
            if s == 1:
                store(t, pair)
                pair = []

    @pl.when(jnp.logical_not(worst < LIMIT))
    def _():
        def block(t, carried):
            pair = []
            for s in range(2):
                top = total = None
                for at in range(0, 4 * chunk, chunk):
                    peak = jnp.max(scores(t, s, at, chunk), axis=1, keepdims=True)
                    top = peak if top is None else jnp.maximum(top, peak)
                for at in range(0, 4 * chunk, chunk):
                    p = jnp.exp2(scores(t, s, at, chunk) - top).astype(BF)
                    part = values(p, s, at, chunk)
                    total = part if total is None else total + part
                pair.append(total / total[:, SUM_LANE:SUM_LANE + 1])
            store(t, pair)
            return carried

        lax.fori_loop(0, 8 // T, block, 0)


def attend(keys, own, other):
    tokens = own.shape[2]
    chunk = 8 * tokens
    b_spec = pl.BlockSpec((8, 2, tokens, chunk), lambda z, p: (0, 0, 0, 0))
    return pl.pallas_call(
        attend_kernel,
        grid=(2, 2),
        in_specs=[
            pl.BlockSpec((8, 1, tokens, LANES), lambda z, p: (0, z, 0, chunk // LANES + p)),
            pl.BlockSpec((1, 2, 4 * chunk, LANES), lambda z, p: (z, p, 0, 0)),
            b_spec,
            b_spec,
        ],
        out_specs=pl.BlockSpec((8, 1, tokens, LANES), lambda z, p: (0, z, 0, p)),
        out_shape=jax.ShapeDtypeStruct((8, 2, tokens, 2 * LANES), BF),
        compiler_params=pltpu.CompilerParams(vmem_limit_bytes=SMALL_VMEM_BYTES),
        cost_estimate=pl.CostEstimate(flops=14_000_000_000, bytes_accessed=10_000_000, transcendentals=13_000_000),
        name="attend",
    )(own, keys, own, other)


def gate_kernel(mod, cn, place, wg, wog, gate_out, og_out):
    samples, tokens, width = mod.shape
    rows = samples * tokens
    og_out[...] = jax.nn.sigmoid(dot(cn[...].reshape(rows, cn.shape[2]), wog[...])).reshape(og_out.shape)
    placed = dot(wg[...], place[...]).astype(BF)
    gate = jax.nn.sigmoid(dot(mod[...].reshape(rows, width), placed))
    gate_out[...] = gate.reshape(gate_out.shape)


def gates(mod, cn, place, wg, wog):
    samples, tokens, width = mod.shape
    return pl.pallas_call(
        gate_kernel,
        out_shape=[
            jax.ShapeDtypeStruct((samples, tokens, HEADS // 2 * LANES), F32),
            jax.ShapeDtypeStruct(mod.shape, F32),
        ],
        compiler_params=pltpu.CompilerParams(vmem_limit_bytes=SMALL_VMEM_BYTES),
        cost_estimate=pl.CostEstimate(flops=32_000_000_000, bytes_accessed=9_000_000, transcendentals=1_000_000),
        name="gates",
    )(mod, cn, place, wg, wog)


def out_kernel(attended, gate, og, act, wo, out, table):
    samples, tokens, width = act.shape
    table[...] = jnp.zeros_like(table)
    for j in range(HEADS // 2):
        table[j * LANES:j * LANES + 96] = wo[j * 96:(j + 1) * 96]
    lane = lax.broadcasted_iota(jnp.int32, (tokens, LANES), 1)
    rows = []
    for s in range(samples):
        lanes = slice(s // 2 * LANES, (s // 2 + 1) * LANES)
        tiles = []
        for j in range(HEADS // 2):
            first = attended[2 * j, :, lanes].astype(F32)
            second = attended[2 * j + 1, :, lanes].astype(F32)
            if s % 2 == 0:
                second = pltpu.roll(second, HEAD, axis=1)
            else:
                first = pltpu.roll(first, 64, axis=1)
                second = pltpu.roll(second, 64 + HEAD, axis=1)
            both = jnp.where(lane < HEAD, first, second)
            tiles.append((both * gate[s, :, j * LANES:(j + 1) * LANES]).astype(BF))
        rows.append(jnp.concatenate(tiles, axis=1))
    projected = dot(jnp.concatenate(rows, axis=0), table[...])
    out[...] = (act[...].astype(F32) + og[...] * projected.reshape(act.shape)).astype(BF)


def project_out(attended, gate, og, act, wo):
    width = act.shape[2]
    return pl.pallas_call(
        out_kernel,
        out_shape=jax.ShapeDtypeStruct(act.shape, BF),
        scratch_shapes=[pltpu.VMEM((HEADS // 2 * LANES, width), BF)],
        compiler_params=pltpu.CompilerParams(vmem_limit_bytes=SMALL_VMEM_BYTES),
        cost_estimate=pl.CostEstimate(flops=2_000_000_000, bytes_accessed=6_000_000, transcendentals=0),
        name="out",
    )(attended, gate, og, act, wo)


def ring(block, step):
    return lax.ppermute(block, "y", [(i, (i + step) % 4) for i in range(4)])


def per_device(
    activations,
    conditioning,
    pair_features,
    key_mask,
    w_scale,
    w_shift,
    w_query,
    w_key,
    w_value,
    w_gate,
    w_out,
    w_outgate,
    w_bias,
):
    tokens = activations.shape[1]
    kv, q, modulated, cond_norm = project_qkv(
        activations, conditioning, key_mask.reshape(1, tokens), w_scale, w_shift, w_query, w_key, w_value
    )
    exchange = lambda a: lax.all_to_all(a, XZ, 0, 0, tiled=True)
    bias = project_bias(pair_features, w_bias.T, q)
    kv, bias = lax.optimization_barrier((exchange(kv), bias))
    up, down = ring(kv, 1), ring(kv, 3)
    own = exchange(bias)
    gate, out_gate = gates(modulated, cond_norm, placement(), w_gate, w_outgate)
    up, down, gate, out_gate = lax.optimization_barrier((up, down, gate, out_gate))
    far = (ring(up[:HEADS // 2], 1), ring(down[HEADS // 2:], 3))
    other = lax.ppermute(own, "co", [(0, 1), (1, 0)])
    place = jnp.stack([lax.axis_index("co"), lax.axis_index("y")]).astype(jnp.int32)
    kv = [a.reshape(-1, 4, 2, tokens, kv.shape[-1]) for a in (kv, up, *far, down)]
    own, other = (a.reshape(8, 2, tokens, own.shape[-1]) for a in (own, other))
    attended = attend(lay_keys(place, kv), own, other)
    attended = exchange(attended.reshape(HEADS, tokens, 2 * LANES))
    return project_out(attended, gate, out_gate, activations, w_out)


def solution(mesh):
    fine = Mesh(mesh.devices.reshape(2, 4, 4, 2, 2), ("zh", "x", "y", "zl", "co"))
    wide, narrow = ("zh", "x", "y"), ("zl", "co")
    in_specs = (
        P(narrow, wide, None),
        P(narrow, wide, None),
        P(wide, narrow, None),
        P(wide),
    ) + (P(),) * 9
    return jax.shard_map(
        per_device, mesh=fine, in_specs=in_specs, out_specs=P(narrow, wide, None), check_vma=False
    )
```

```python
import math

import jax
import jax.numpy as jnp
import numpy as np
from jax import lax
from jax.experimental import pallas as pl
from jax.experimental.pallas import tpu as pltpu
from jax.sharding import Mesh, PartitionSpec as P

EPSILON = 1e-05
NEGATIVE = -1e30
LOG2E = math.log2(math.e)
HEADS = 16
HEAD = 48
LANES = 128
GROUP = 16
MARK_LANE = 95
PAD_LANE = 96
SUM_LANE = 97
XZ = ("zh", "x", "zl")
BF = jnp.bfloat16
F32 = jnp.float32
VMEM_BYTES = 56 * 1024 * 1024
SMALL_VMEM_BYTES = 40 * 1024 * 1024
NT = (((1,), (1,)), ((), ()))


def layer_norm(entries):
    entries = entries.astype(F32)
    row_mean = jnp.mean(entries, axis=-1, keepdims=True)
    centered = entries - row_mean
    variance = jnp.mean(centered * centered, axis=-1, keepdims=True)
    return centered * lax.rsqrt(variance + EPSILON)


def dot(left, right):
    return jnp.dot(left, right, preferred_element_type=F32)


def placement():
    pairs = np.zeros((HEADS // 2, 2 * HEAD, HEADS // 2, LANES), np.float32)
    for pair in range(HEADS // 2):
        for channel in range(2 * HEAD):
            pairs[pair, channel, pair, channel] = 1
    return jnp.asarray(pairs.reshape(HEADS * HEAD, HEADS // 2 * LANES), BF)


def moved(columns, rows, head, to, lane):
    tile, offset = divmod(head * HEAD, LANES)
    shift = (to - offset) % LANES
    take = lambda i: columns[rows, i * LANES:(i + 1) * LANES]
    turn = lambda x: pltpu.roll(x, shift, axis=1) if shift else x
    first = turn(take(tile))
    if offset + HEAD <= LANES:
        return first
    return jnp.where(lane < to + LANES - offset, first, turn(take(tile + 1)))


def qkv_kernel(act, cond, mask, ws, wsh, wq, wk, wv, kv_out, q_out, mod_out, cn_out, mod):
    samples, tokens, width = act.shape
    rows = samples * tokens

    @pl.when(pl.program_id(0) == 0)
    def _():
        cond_norm = layer_norm(cond[...].reshape(rows, cond.shape[2])).astype(BF)
        normed = layer_norm(act[...].reshape(rows, width))
        modulated = jax.nn.sigmoid(dot(cond_norm, ws[...])) * normed + dot(cond_norm, wsh[...])
        mod[...] = modulated.astype(BF)
        mod_out[...] = mod[...].reshape(mod_out.shape)
        cn_out[...] = cond_norm.reshape(cn_out.shape)

    modulated = mod[...]
    lane = lax.broadcasted_iota(jnp.int32, (tokens, LANES), 1)
    square = (tokens, tokens)
    diagonal = lax.broadcasted_iota(jnp.int32, square, 0) == lax.broadcasted_iota(jnp.int32, square, 1)
    padded = jnp.broadcast_to(jnp.where(mask[...] > 0, 0.0, 1.0), square)
    padded = jnp.sum(jnp.where(diagonal, padded, 0.0), axis=1, keepdims=True)
    marked = (lane == MARK_LANE) & (padded > 0.5)
    sample = [slice(s * tokens, (s + 1) * tokens) for s in range(samples)]
    k = dot(modulated, wk[...])
    v = dot(modulated, wv[...])
    for h in range(GROUP):
        tile = [
            jnp.where(lane < HEAD, moved(k, row, h, 0, lane), moved(v, row, h, HEAD, lane)) for row in sample
        ]
        for s in range(3):
            spare = pltpu.roll(tile[3], 96 - 32 * s, axis=1)
            merged = jnp.where(lane < 96, tile[s], spare)
            if s == 0:
                merged = jnp.where(marked, NEGATIVE, merged)
            kv_out[h, :, s * LANES:(s + 1) * LANES] = merged.astype(BF)
    q = dot(modulated, wq[...]) * (LOG2E / math.sqrt(HEAD))
    for h in range(GROUP):
        for p in range(samples // 2):
            first = moved(q, sample[2 * p], h, 0, lane)
            second = moved(q, sample[2 * p + 1], h, 64, lane)
            q_out[h, :, p * LANES:(p + 1) * LANES] = jnp.where(lane < 64, first, second).astype(BF)


def project_qkv(act, cond, mask, ws, wsh, wq, wk, wv):
    samples, tokens, width = act.shape
    steps = HEADS // GROUP
    columns = GROUP * HEAD
    whole = lambda a: pl.BlockSpec(a.shape, lambda g: (0,) * a.ndim)
    part = pl.BlockSpec((width, columns), lambda g: (0, g))
    return pl.pallas_call(
        qkv_kernel,
        grid=(steps,),
        in_specs=[whole(act), whole(cond), whole(mask), whole(ws), whole(wsh), part, part, part],
        out_specs=[
            pl.BlockSpec((GROUP, tokens, 3 * LANES), lambda g: (g, 0, 0)),
            pl.BlockSpec((GROUP, tokens, 2 * LANES), lambda g: (g, 0, 0)),
            whole(act),
            whole(cond),
        ],
        out_shape=[
            jax.ShapeDtypeStruct((HEADS, tokens, 3 * LANES), BF),
            jax.ShapeDtypeStruct((HEADS, tokens, 2 * LANES), BF),
            jax.ShapeDtypeStruct(act.shape, BF),
            jax.ShapeDtypeStruct(cond.shape, BF),
        ],
        scratch_shapes=[pltpu.VMEM((samples * tokens, width), BF)],
        compiler_params=pltpu.CompilerParams(vmem_limit_bytes=VMEM_BYTES),
        cost_estimate=pl.CostEstimate(flops=4_000_000_000, bytes_accessed=10_000_000, transcendentals=300_000),
        name="qkv",
    )(act, cond, mask, ws, wsh, wq, wk, wv)


def bias_kernel(pair, w_bias, q, out, rows):
    count, keys, channels = pair.shape
    wt = w_bias[...]
    zero = jnp.zeros((HEADS, channels), BF)
    part = jnp.full((HEADS, channels), 1.0 / channels, BF)
    weights = jnp.concatenate(
        [jnp.concatenate([wt, zero], axis=1), jnp.concatenate([zero, part], axis=1)], axis=0
    )
    for i in range(count):
        x = pair[i].astype(F32)
        c = (x - jnp.mean(x, axis=1, keepdims=True)).astype(BF)
        both = jnp.concatenate([c, c * c], axis=1)
        r = lax.dot_general(weights, both, NT, preferred_element_type=F32)
        rows[i] = r[:HEADS] * (lax.rsqrt(r[HEADS:] + EPSILON) * LOG2E)
    out[:, :, :keys] = jnp.swapaxes(rows[...], 0, 1).astype(BF)
    out[:, :, keys:] = q[...]


def project_bias(pair, w_bias, q):
    queries, keys, channels = pair.shape
    step = 16
    extent = keys + q.shape[2]
    return pl.pallas_call(
        bias_kernel,
        grid=(queries // step,),
        in_specs=[
            pl.BlockSpec((step, keys, channels), lambda i: (i, 0, 0)),
            pl.BlockSpec(w_bias.shape, lambda i: (0, 0)),
            pl.BlockSpec((HEADS, step, q.shape[2]), lambda i: (0, i, 0)),
        ],
        out_specs=pl.BlockSpec((HEADS, step, extent), lambda i: (0, i, 0)),
        out_shape=jax.ShapeDtypeStruct((HEADS, queries, extent), BF),
        scratch_shapes=[pltpu.VMEM((step, HEADS, keys), F32)],
        compiler_params=pltpu.CompilerParams(vmem_limit_bytes=VMEM_BYTES),
        cost_estimate=pl.CostEstimate(flops=10_000_000_000, bytes_accessed=15_000_000, transcendentals=100_000),
        name="bias",
    )(pair, w_bias, q)


T = 4
PIECE = 128
LIMIT = 2.0**100


def lay_kernel(place, near, up, far_low, far_high, down, keys):
    tokens = near.shape[-2]
    core, row = place[0], place[1]
    lane = lax.broadcasted_iota(jnp.int32, (tokens, LANES), 1)
    for z in range(2):
        parts = (near.at[z], up.at[z], (far_low, far_high)[z].at[0], down.at[z])
        for o in range(2):
            quarter = core if o == 0 else 1 - core
            for low in range(2):
                for step, part in enumerate(parts):
                    block = (z * 2 + o) * 8 + low * 4 + lax.rem(row + 4 - step, 4)
                    at = pl.ds(pl.multiple_of(block * tokens, 16), tokens)
                    tiles = [part[2 * quarter + low, 0, :, i * LANES:(i + 1) * LANES] for i in range(3)]
                    wide = [t.astype(F32) for t in tiles]
                    mark = pltpu.roll(wide[0], PAD_LANE - MARK_LANE, axis=1)
                    pad = jnp.where(mark < 0.5 * NEGATIVE, NEGATIVE, 0.0)
                    tail = jnp.where(lane == PAD_LANE, pad, jnp.where(lane == SUM_LANE, 1.0, 0.0)).astype(BF)
                    for s in range(3):
                        keys[0, s, at] = jnp.where(lane < 96, tiles[s], tail)
                    last = jnp.where(
                        lane < 32,
                        pltpu.roll(wide[0], 32, axis=1),
                        jnp.where(lane < 64, pltpu.roll(wide[1], 64, axis=1), pltpu.roll(wide[2], 96, axis=1)),
                    ).astype(BF)
                    keys[0, 3, at] = jnp.where(lane < 96, last, tail)


def lay_keys(place, kv):
    tokens = kv[0].shape[3]
    extent = 32 * tokens
    return pl.pallas_call(
        lay_kernel,
        grid_spec=pltpu.PrefetchScalarGridSpec(
            num_scalar_prefetch=1,
            grid=(2,),
            in_specs=[pl.BlockSpec((a.shape[0], 4, 1, tokens, 3 * LANES), lambda z, c: (0, 0, z, 0, 0)) for a in kv],
            out_specs=pl.BlockSpec((1, 4, extent, LANES), lambda z, c: (z, 0, 0, 0)),
        ),
        out_shape=jax.ShapeDtypeStruct((2, 4, extent, LANES), BF),
        compiler_params=pltpu.CompilerParams(vmem_limit_bytes=SMALL_VMEM_BYTES),
        cost_estimate=pl.CostEstimate(flops=40_000_000_000, bytes_accessed=10_000_000, transcendentals=0),
        name="lay",
    )(place, *kv)


def attend_kernel(q, keys, own, other, out):
    tokens = q.shape[2]
    chunk = 8 * tokens
    span = T * tokens
    lane = lax.broadcasted_iota(jnp.int32, (span, LANES), 1)
    pad_one = jnp.where(lane == PAD_LANE, 1.0, 0.0).astype(BF)

    def query(t, s):
        pair_q = q[pl.ds(t * T, T), 0].reshape(span, LANES)
        if s == 1:
            pair_q = pltpu.roll(pair_q.astype(F32), 64, axis=1).astype(BF)
        return jnp.where(lane < HEAD, pair_q, pad_one)

    def scores(mine, t, s, at, width):
        part = lax.dot_general(mine, keys[0, s, at:at + width], NT, preferred_element_type=F32)
        columns = at % chunk
        bias = own if at // chunk % 2 == 0 else other
        bias = bias[pl.ds(t * T, T), at // chunk // 2, :, columns:columns + width].reshape(span, width)
        return part + bias.astype(F32)

    def values(p, s, at, width):
        return dot(p, keys[0, s, at:at + width])

    def store(t, pair):
        low = pltpu.roll(pair[0], LANES - HEAD, axis=1)
        high = pltpu.roll(pair[1], 64 - HEAD, axis=1)
        merged = jnp.where(lane < 64, low, high).astype(BF)
        out[pl.ds(t * T, T), 0] = merged.reshape(T, tokens, LANES)

    pieces = [(t, s, at) for t in range(8 // T) for s in range(2) for at in range(0, 4 * chunk, PIECE)]
    mine = {block: query(*block) for block in {piece[:2]: None for piece in pieces}}
    following = scores(mine[pieces[0][:2]], *pieces[0], PIECE)
    top, total, pair, worst = None, None, [], jnp.float32(0.0)
    for i, (t, s, at) in enumerate(pieces):
        current = following
        if at == 0:
            top, total = jnp.max(current, axis=1, keepdims=True), None
        if i + 1 < len(pieces):
            following = scores(mine[pieces[i + 1][:2]], *pieces[i + 1], PIECE)
        part = values(jnp.exp2(current - top).astype(BF), s, at, PIECE)
        total = part if total is None else total + part
        if at == 4 * chunk - PIECE:
            weight = total[:, SUM_LANE:SUM_LANE + 1]
            worst = jnp.maximum(worst, jnp.max(weight))
            pair.append(total / weight)
            if s == 1:
                store(t, pair)
                pair = []

    @pl.when(jnp.logical_not(worst < LIMIT))
    def _():
        def block(t, carried):
            pair = []
            for s in range(2):
                top = total = None
                row = query(t, s)
                for at in range(0, 4 * chunk, chunk):
                    peak = jnp.max(scores(row, t, s, at, chunk), axis=1, keepdims=True)
                    top = peak if top is None else jnp.maximum(top, peak)
                for at in range(0, 4 * chunk, chunk):
                    p = jnp.exp2(scores(row, t, s, at, chunk) - top).astype(BF)
                    part = values(p, s, at, chunk)
                    total = part if total is None else total + part
                pair.append(total / total[:, SUM_LANE:SUM_LANE + 1])
            store(t, pair)
            return carried

        lax.fori_loop(0, 8 // T, block, 0)


def attend(keys, own, other):
    tokens = own.shape[2]
    chunk = 8 * tokens
    b_spec = pl.BlockSpec((8, 2, tokens, chunk), lambda z, p: (0, 0, 0, 0))
    return pl.pallas_call(
        attend_kernel,
        grid=(2, 2),
        in_specs=[
            pl.BlockSpec((8, 1, tokens, LANES), lambda z, p: (0, z, 0, chunk // LANES + p)),
            pl.BlockSpec((1, 2, 4 * chunk, LANES), lambda z, p: (z, p, 0, 0)),
            b_spec,
            b_spec,
        ],
        out_specs=pl.BlockSpec((8, 1, tokens, LANES), lambda z, p: (0, z, 0, p)),
        out_shape=jax.ShapeDtypeStruct((8, 2, tokens, 2 * LANES), BF),
        compiler_params=pltpu.CompilerParams(vmem_limit_bytes=SMALL_VMEM_BYTES),
        cost_estimate=pl.CostEstimate(flops=14_000_000_000, bytes_accessed=10_000_000, transcendentals=13_000_000),
        name="attend",
    )(own, keys, own, other)


def gate_kernel(mod, cn, place, wg, wog, gate_out, og_out):
    samples, tokens, width = mod.shape
    rows = samples * tokens
    og_out[...] = jax.nn.sigmoid(dot(cn[...].reshape(rows, cn.shape[2]), wog[...])).reshape(og_out.shape)
    placed = dot(wg[...], place[...]).astype(BF)
    gate = jax.nn.sigmoid(dot(mod[...].reshape(rows, width), placed))
    gate_out[...] = gate.reshape(gate_out.shape)


def gates(mod, cn, place, wg, wog):
    samples, tokens, width = mod.shape
    return pl.pallas_call(
        gate_kernel,
        out_shape=[
            jax.ShapeDtypeStruct((samples, tokens, HEADS // 2 * LANES), F32),
            jax.ShapeDtypeStruct(mod.shape, F32),
        ],
        compiler_params=pltpu.CompilerParams(vmem_limit_bytes=SMALL_VMEM_BYTES),
        cost_estimate=pl.CostEstimate(flops=32_000_000_000, bytes_accessed=9_000_000, transcendentals=1_000_000),
        name="gates",
    )(mod, cn, place, wg, wog)


def out_kernel(attended, gate, og, act, wo, out, table):
    samples, tokens, width = act.shape
    table[...] = jnp.zeros_like(table)
    for j in range(HEADS // 2):
        table[j * LANES:j * LANES + 96] = wo[j * 96:(j + 1) * 96]
    lane = lax.broadcasted_iota(jnp.int32, (tokens, LANES), 1)
    rows = []
    for s in range(samples):
        lanes = slice(s // 2 * LANES, (s // 2 + 1) * LANES)
        tiles = []
        for j in range(HEADS // 2):
            first = attended[2 * j, :, lanes].astype(F32)
            second = attended[2 * j + 1, :, lanes].astype(F32)
            if s % 2 == 0:
                second = pltpu.roll(second, HEAD, axis=1)
            else:
                first = pltpu.roll(first, 64, axis=1)
                second = pltpu.roll(second, 64 + HEAD, axis=1)
            both = jnp.where(lane < HEAD, first, second)
            tiles.append((both * gate[s, :, j * LANES:(j + 1) * LANES]).astype(BF))
        rows.append(jnp.concatenate(tiles, axis=1))
    projected = dot(jnp.concatenate(rows, axis=0), table[...])
    out[...] = (act[...].astype(F32) + og[...] * projected.reshape(act.shape)).astype(BF)


def project_out(attended, gate, og, act, wo):
    width = act.shape[2]
    return pl.pallas_call(
        out_kernel,
        out_shape=jax.ShapeDtypeStruct(act.shape, BF),
        scratch_shapes=[pltpu.VMEM((HEADS // 2 * LANES, width), BF)],
        compiler_params=pltpu.CompilerParams(vmem_limit_bytes=SMALL_VMEM_BYTES),
        cost_estimate=pl.CostEstimate(flops=2_000_000_000, bytes_accessed=6_000_000, transcendentals=0),
        name="out",
    )(attended, gate, og, act, wo)


def halves_kernel(first, second, first_out, second_out):
    first_out[...] = first[...]
    second_out[...] = second[...]


def halves(first, second):
    block = (first.shape[0] // 2,) + first.shape[1:]
    low = pl.BlockSpec(block, lambda i: (0, 0, 0))
    high = pl.BlockSpec(block, lambda i: (1, 0, 0))
    return pl.pallas_call(
        halves_kernel,
        grid=(1,),
        in_specs=[low, high],
        out_specs=[low, low],
        out_shape=[jax.ShapeDtypeStruct(block, first.dtype)] * 2,
        compiler_params=pltpu.CompilerParams(vmem_limit_bytes=SMALL_VMEM_BYTES),
        cost_estimate=pl.CostEstimate(flops=0, bytes_accessed=2_000_000, transcendentals=0),
        name="halves",
    )(first, second)


def ring(block, step):
    return lax.ppermute(block, "y", [(i, (i + step) % 4) for i in range(4)])


def per_device(
    activations,
    conditioning,
    pair_features,
    key_mask,
    w_scale,
    w_shift,
    w_query,
    w_key,
    w_value,
    w_gate,
    w_out,
    w_outgate,
    w_bias,
):
    tokens = activations.shape[1]
    kv, q, modulated, cond_norm = project_qkv(
        activations, conditioning, key_mask.reshape(1, tokens), w_scale, w_shift, w_query, w_key, w_value
    )
    exchange = lambda a: lax.all_to_all(a, XZ, 0, 0, tiled=True)
    bias = project_bias(pair_features, w_bias.T, q)
    kv, bias = lax.optimization_barrier((exchange(kv), bias))
    up, down = ring(kv, 1), ring(kv, 3)
    own = exchange(bias)
    gate, out_gate = gates(modulated, cond_norm, placement(), w_gate, w_outgate)
    up, down, gate, out_gate = lax.optimization_barrier((up, down, gate, out_gate))
    up_half, down_half = halves(up, down)
    far = (ring(up_half, 1), ring(down_half, 3))
    other = lax.ppermute(own, "co", [(0, 1), (1, 0)])
    place = jnp.stack([lax.axis_index("co"), lax.axis_index("y")]).astype(jnp.int32)
    kv = [a.reshape(-1, 4, 2, tokens, kv.shape[-1]) for a in (kv, up, *far, down)]
    own, other = (a.reshape(8, 2, tokens, own.shape[-1]) for a in (own, other))
    attended = attend(lay_keys(place, kv), own, other)
    attended = exchange(attended.reshape(HEADS, tokens, 2 * LANES))
    return project_out(attended, gate, out_gate, activations, w_out)


def solution(mesh):
    fine = Mesh(mesh.devices.reshape(2, 4, 4, 2, 2), ("zh", "x", "y", "zl", "co"))
    wide, narrow = ("zh", "x", "y"), ("zl", "co")
    in_specs = (
        P(narrow, wide, None),
        P(narrow, wide, None),
        P(wide, narrow, None),
        P(wide),
    ) + (P(),) * 9
    return jax.shard_map(
        per_device, mesh=fine, in_specs=in_specs, out_specs=P(narrow, wide, None), check_vma=False
    )
```

```python
import math

import jax
import jax.numpy as jnp
import numpy as np
from jax import lax
from jax.experimental import pallas as pl
from jax.experimental.pallas import tpu as pltpu
from jax.sharding import Mesh, PartitionSpec as P

EPSILON = 1e-05
NEGATIVE = -1e30
LOG2E = math.log2(math.e)
HEADS = 16
HEAD = 48
LANES = 128
GROUP = 16
MARK_LANE = 95
PAD_LANE = 96
SUM_LANE = 97
XZ = ("zh", "x", "zl")
BF = jnp.bfloat16
F32 = jnp.float32
VMEM_BYTES = 56 * 1024 * 1024
SMALL_VMEM_BYTES = 40 * 1024 * 1024
NT = (((1,), (1,)), ((), ()))


def layer_norm(entries):
    entries = entries.astype(F32)
    row_mean = jnp.mean(entries, axis=-1, keepdims=True)
    centered = entries - row_mean
    variance = jnp.mean(centered * centered, axis=-1, keepdims=True)
    return centered * lax.rsqrt(variance + EPSILON)


def dot(left, right):
    return jnp.dot(left, right, preferred_element_type=F32)


def placement():
    pairs = np.zeros((HEADS // 2, 2 * HEAD, HEADS // 2, LANES), np.float32)
    for pair in range(HEADS // 2):
        for channel in range(2 * HEAD):
            pairs[pair, channel, pair, channel] = 1
    return jnp.asarray(pairs.reshape(HEADS * HEAD, HEADS // 2 * LANES), BF)


def moved(columns, rows, head, to, lane):
    tile, offset = divmod(head * HEAD, LANES)
    shift = (to - offset) % LANES
    take = lambda i: columns[rows, i * LANES:(i + 1) * LANES]
    turn = lambda x: pltpu.roll(x, shift, axis=1) if shift else x
    first = turn(take(tile))
    if offset + HEAD <= LANES:
        return first
    return jnp.where(lane < to + LANES - offset, first, turn(take(tile + 1)))


def qkv_kernel(act, cond, mask, ws, wsh, wq, wk, wv, kv_out, q_out, mod_out, cn_out, mod):
    samples, tokens, width = act.shape
    rows = samples * tokens

    @pl.when(pl.program_id(0) == 0)
    def _():
        cond_norm = layer_norm(cond[...].reshape(rows, cond.shape[2])).astype(BF)
        normed = layer_norm(act[...].reshape(rows, width))
        modulated = jax.nn.sigmoid(dot(cond_norm, ws[...])) * normed + dot(cond_norm, wsh[...])
        mod[...] = modulated.astype(BF)
        mod_out[...] = mod[...].reshape(mod_out.shape)
        cn_out[...] = cond_norm.reshape(cn_out.shape)

    modulated = mod[...]
    lane = lax.broadcasted_iota(jnp.int32, (tokens, LANES), 1)
    square = (tokens, tokens)
    diagonal = lax.broadcasted_iota(jnp.int32, square, 0) == lax.broadcasted_iota(jnp.int32, square, 1)
    padded = jnp.broadcast_to(jnp.where(mask[...] > 0, 0.0, 1.0), square)
    padded = jnp.sum(jnp.where(diagonal, padded, 0.0), axis=1, keepdims=True)
    marked = (lane == MARK_LANE) & (padded > 0.5)
    sample = [slice(s * tokens, (s + 1) * tokens) for s in range(samples)]
    k = dot(modulated, wk[...])
    v = dot(modulated, wv[...])
    for h in range(GROUP):
        tile = [
            jnp.where(lane < HEAD, moved(k, row, h, 0, lane), moved(v, row, h, HEAD, lane)) for row in sample
        ]
        for s in range(3):
            spare = pltpu.roll(tile[3], 96 - 32 * s, axis=1)
            merged = jnp.where(lane < 96, tile[s], spare)
            if s == 0:
                merged = jnp.where(marked, NEGATIVE, merged)
            kv_out[h, :, s * LANES:(s + 1) * LANES] = merged.astype(BF)
    q = dot(modulated, wq[...]) * (LOG2E / math.sqrt(HEAD))
    for h in range(GROUP):
        for p in range(samples // 2):
            first = moved(q, sample[2 * p], h, 0, lane)
            second = moved(q, sample[2 * p + 1], h, 64, lane)
            q_out[h, :, p * LANES:(p + 1) * LANES] = jnp.where(lane < 64, first, second).astype(BF)


def project_qkv(act, cond, mask, ws, wsh, wq, wk, wv):
    samples, tokens, width = act.shape
    steps = HEADS // GROUP
    columns = GROUP * HEAD
    whole = lambda a: pl.BlockSpec(a.shape, lambda g: (0,) * a.ndim)
    part = pl.BlockSpec((width, columns), lambda g: (0, g))
    return pl.pallas_call(
        qkv_kernel,
        grid=(steps,),
        in_specs=[whole(act), whole(cond), whole(mask), whole(ws), whole(wsh), part, part, part],
        out_specs=[
            pl.BlockSpec((GROUP, tokens, 3 * LANES), lambda g: (g, 0, 0)),
            pl.BlockSpec((GROUP, tokens, 2 * LANES), lambda g: (g, 0, 0)),
            whole(act),
            whole(cond),
        ],
        out_shape=[
            jax.ShapeDtypeStruct((HEADS, tokens, 3 * LANES), BF),
            jax.ShapeDtypeStruct((HEADS, tokens, 2 * LANES), BF),
            jax.ShapeDtypeStruct(act.shape, BF),
            jax.ShapeDtypeStruct(cond.shape, BF),
        ],
        scratch_shapes=[pltpu.VMEM((samples * tokens, width), BF)],
        compiler_params=pltpu.CompilerParams(vmem_limit_bytes=VMEM_BYTES),
        cost_estimate=pl.CostEstimate(flops=4_000_000_000, bytes_accessed=10_000_000, transcendentals=300_000),
        name="qkv",
    )(act, cond, mask, ws, wsh, wq, wk, wv)


def bias_kernel(pair, w_bias, q, out, rows):
    count, keys, channels = pair.shape
    wt = w_bias[...]
    zero = jnp.zeros((HEADS, channels), BF)
    part = jnp.full((HEADS, channels), 1.0 / channels, BF)
    weights = jnp.concatenate(
        [jnp.concatenate([wt, zero], axis=1), jnp.concatenate([zero, part], axis=1)], axis=0
    )
    for i in range(count):
        x = pair[i].astype(F32)
        c = (x - jnp.mean(x, axis=1, keepdims=True)).astype(BF)
        both = jnp.concatenate([c, c * c], axis=1)
        r = lax.dot_general(weights, both, NT, preferred_element_type=F32)
        rows[i] = r[:HEADS] * (lax.rsqrt(r[HEADS:] + EPSILON) * LOG2E)
    out[:, :, :keys] = jnp.swapaxes(rows[...], 0, 1).astype(BF)
    out[:, :, keys:] = q[...]


def project_bias(pair, w_bias, q):
    queries, keys, channels = pair.shape
    step = 16
    extent = keys + q.shape[2]
    return pl.pallas_call(
        bias_kernel,
        grid=(queries // step,),
        in_specs=[
            pl.BlockSpec((step, keys, channels), lambda i: (i, 0, 0)),
            pl.BlockSpec(w_bias.shape, lambda i: (0, 0)),
            pl.BlockSpec((HEADS, step, q.shape[2]), lambda i: (0, i, 0)),
        ],
        out_specs=pl.BlockSpec((HEADS, step, extent), lambda i: (0, i, 0)),
        out_shape=jax.ShapeDtypeStruct((HEADS, queries, extent), BF),
        scratch_shapes=[pltpu.VMEM((step, HEADS, keys), F32)],
        compiler_params=pltpu.CompilerParams(vmem_limit_bytes=VMEM_BYTES),
        cost_estimate=pl.CostEstimate(flops=10_000_000_000, bytes_accessed=15_000_000, transcendentals=100_000),
        name="bias",
    )(pair, w_bias, q)


T = 4
PIECE = 128
LIMIT = 2.0**100


def lay_kernel(place, near, up, far_low, far_high, down, keys):
    tokens = near.shape[-2]
    core, row = place[0], place[1]
    lane = lax.broadcasted_iota(jnp.int32, (tokens, LANES), 1)
    for z in range(2):
        parts = (near.at[z], up.at[z], (far_low, far_high)[z].at[0], down.at[z])
        for o in range(2):
            quarter = core if o == 0 else 1 - core
            for low in range(2):
                for step, part in enumerate(parts):
                    block = (z * 2 + o) * 8 + low * 4 + lax.rem(row + 4 - step, 4)
                    at = pl.ds(pl.multiple_of(block * tokens, 16), tokens)
                    tiles = [part[2 * quarter + low, 0, :, i * LANES:(i + 1) * LANES] for i in range(3)]
                    wide = [t.astype(F32) for t in tiles]
                    mark = pltpu.roll(wide[0], PAD_LANE - MARK_LANE, axis=1)
                    pad = jnp.where(mark < 0.5 * NEGATIVE, NEGATIVE, 0.0)
                    tail = jnp.where(lane == PAD_LANE, pad, jnp.where(lane == SUM_LANE, 1.0, 0.0)).astype(BF)
                    for s in range(3):
                        keys[0, s, at] = jnp.where(lane < 96, tiles[s], tail)
                    last = jnp.where(
                        lane < 32,
                        pltpu.roll(wide[0], 32, axis=1),
                        jnp.where(lane < 64, pltpu.roll(wide[1], 64, axis=1), pltpu.roll(wide[2], 96, axis=1)),
                    ).astype(BF)
                    keys[0, 3, at] = jnp.where(lane < 96, last, tail)


def lay_keys(place, kv):
    tokens = kv[0].shape[3]
    extent = 32 * tokens
    return pl.pallas_call(
        lay_kernel,
        grid_spec=pltpu.PrefetchScalarGridSpec(
            num_scalar_prefetch=1,
            grid=(2,),
            in_specs=[pl.BlockSpec((a.shape[0], 4, 1, tokens, 3 * LANES), lambda z, c: (0, 0, z, 0, 0)) for a in kv],
            out_specs=pl.BlockSpec((1, 4, extent, LANES), lambda z, c: (z, 0, 0, 0)),
        ),
        out_shape=jax.ShapeDtypeStruct((2, 4, extent, LANES), BF),
        compiler_params=pltpu.CompilerParams(vmem_limit_bytes=SMALL_VMEM_BYTES),
        cost_estimate=pl.CostEstimate(flops=40_000_000_000, bytes_accessed=10_000_000, transcendentals=0),
        name="lay",
    )(place, *kv)


def attend_kernel(q, keys, own, other, out):
    tokens = q.shape[2]
    chunk = 8 * tokens
    span = T * tokens
    lane = lax.broadcasted_iota(jnp.int32, (span, LANES), 1)
    pad_one = jnp.where(lane == PAD_LANE, 1.0, 0.0).astype(BF)

    def query(t, s):
        pair_q = q[pl.ds(t * T, T), 0].reshape(span, LANES)
        if s == 1:
            pair_q = pltpu.roll(pair_q.astype(F32), 64, axis=1).astype(BF)
        return jnp.where(lane < HEAD, pair_q, pad_one)

    def scores(mine, t, s, at, width):
        part = lax.dot_general(mine, keys[0, s, at:at + width], NT, preferred_element_type=F32)
        columns = at % chunk
        bias = own if at // chunk % 2 == 0 else other
        bias = bias[pl.ds(t * T, T), at // chunk // 2, :, columns:columns + width].reshape(span, width)
        return part + bias.astype(F32)

    def values(p, s, at, width):
        return dot(p, keys[0, s, at:at + width])

    def store(t, pair):
        low = pltpu.roll(pair[0], LANES - HEAD, axis=1)
        high = pltpu.roll(pair[1], 64 - HEAD, axis=1)
        merged = jnp.where(lane < 64, low, high).astype(BF)
        out[pl.ds(t * T, T), 0] = merged.reshape(T, tokens, LANES)

    pieces = [(t, s, at) for t in range(8 // T) for s in range(2) for at in range(0, 4 * chunk, PIECE)]
    mine = {block: query(*block) for block in {piece[:2]: None for piece in pieces}}
    following = scores(mine[pieces[0][:2]], *pieces[0], PIECE)
    top, total, pair, worst = None, None, [], jnp.float32(0.0)
    for i, (t, s, at) in enumerate(pieces):
        current = following
        if at == 0:
            top, total = jnp.max(current, axis=1, keepdims=True), None
        if i + 1 < len(pieces):
            following = scores(mine[pieces[i + 1][:2]], *pieces[i + 1], PIECE)
        part = values(jnp.exp2(current - top).astype(BF), s, at, PIECE)
        total = part if total is None else total + part
        if at == 4 * chunk - PIECE:
            weight = total[:, SUM_LANE:SUM_LANE + 1]
            worst = jnp.maximum(worst, jnp.max(weight))
            pair.append(total / weight)
            if s == 1:
                store(t, pair)
                pair = []

    @pl.when(jnp.logical_not(worst < LIMIT))
    def _():
        def block(t, carried):
            pair = []
            for s in range(2):
                top = total = None
                row = query(t, s)
                for at in range(0, 4 * chunk, chunk):
                    peak = jnp.max(scores(row, t, s, at, chunk), axis=1, keepdims=True)
                    top = peak if top is None else jnp.maximum(top, peak)
                for at in range(0, 4 * chunk, chunk):
                    p = jnp.exp2(scores(row, t, s, at, chunk) - top).astype(BF)
                    part = values(p, s, at, chunk)
                    total = part if total is None else total + part
                pair.append(total / total[:, SUM_LANE:SUM_LANE + 1])
            store(t, pair)
            return carried

        lax.fori_loop(0, 8 // T, block, 0)


def attend(keys, own, other):
    tokens = own.shape[2]
    chunk = 8 * tokens
    b_spec = pl.BlockSpec(memory_space=pltpu.VMEM)
    return pl.pallas_call(
        attend_kernel,
        grid=(2, 2),
        in_specs=[
            pl.BlockSpec((8, 1, tokens, LANES), lambda z, p: (0, z, 0, chunk // LANES + p)),
            pl.BlockSpec((1, 2, 4 * chunk, LANES), lambda z, p: (z, p, 0, 0)),
            b_spec,
            b_spec,
        ],
        out_specs=pl.BlockSpec((8, 1, tokens, LANES), lambda z, p: (0, z, 0, p)),
        out_shape=jax.ShapeDtypeStruct((8, 2, tokens, 2 * LANES), BF),
        compiler_params=pltpu.CompilerParams(vmem_limit_bytes=SMALL_VMEM_BYTES),
        cost_estimate=pl.CostEstimate(flops=14_000_000_000, bytes_accessed=10_000_000, transcendentals=13_000_000),
        name="attend",
    )(own, keys, own, other)


def gate_kernel(mod, cn, place, wg, wog, gate_out, og_out):
    samples, tokens, width = mod.shape
    rows = samples * tokens
    og_out[...] = jax.nn.sigmoid(dot(cn[...].reshape(rows, cn.shape[2]), wog[...])).reshape(og_out.shape)
    placed = dot(wg[...], place[...]).astype(BF)
    gate = jax.nn.sigmoid(dot(mod[...].reshape(rows, width), placed))
    gate_out[...] = gate.reshape(gate_out.shape)


def gates(mod, cn, place, wg, wog):
    samples, tokens, width = mod.shape
    return pl.pallas_call(
        gate_kernel,
        out_shape=[
            jax.ShapeDtypeStruct((samples, tokens, HEADS // 2 * LANES), F32),
            jax.ShapeDtypeStruct(mod.shape, F32),
        ],
        compiler_params=pltpu.CompilerParams(vmem_limit_bytes=SMALL_VMEM_BYTES),
        cost_estimate=pl.CostEstimate(flops=32_000_000_000, bytes_accessed=9_000_000, transcendentals=1_000_000),
        name="gates",
    )(mod, cn, place, wg, wog)


def out_kernel(attended, gate, og, act, wo, out, table):
    samples, tokens, width = act.shape
    table[...] = jnp.zeros_like(table)
    for j in range(HEADS // 2):
        table[j * LANES:j * LANES + 96] = wo[j * 96:(j + 1) * 96]
    lane = lax.broadcasted_iota(jnp.int32, (tokens, LANES), 1)
    rows = []
    for s in range(samples):
        lanes = slice(s // 2 * LANES, (s // 2 + 1) * LANES)
        tiles = []
        for j in range(HEADS // 2):
            first = attended[2 * j, :, lanes].astype(F32)
            second = attended[2 * j + 1, :, lanes].astype(F32)
            if s % 2 == 0:
                second = pltpu.roll(second, HEAD, axis=1)
            else:
                first = pltpu.roll(first, 64, axis=1)
                second = pltpu.roll(second, 64 + HEAD, axis=1)
            both = jnp.where(lane < HEAD, first, second)
            tiles.append((both * gate[s, :, j * LANES:(j + 1) * LANES]).astype(BF))
        rows.append(jnp.concatenate(tiles, axis=1))
    projected = dot(jnp.concatenate(rows, axis=0), table[...])
    out[...] = (act[...].astype(F32) + og[...] * projected.reshape(act.shape)).astype(BF)


def project_out(attended, gate, og, act, wo):
    width = act.shape[2]
    return pl.pallas_call(
        out_kernel,
        out_shape=jax.ShapeDtypeStruct(act.shape, BF),
        scratch_shapes=[pltpu.VMEM((HEADS // 2 * LANES, width), BF)],
        compiler_params=pltpu.CompilerParams(vmem_limit_bytes=SMALL_VMEM_BYTES),
        cost_estimate=pl.CostEstimate(flops=2_000_000_000, bytes_accessed=6_000_000, transcendentals=0),
        name="out",
    )(attended, gate, og, act, wo)


def halves_kernel(first, second, first_out, second_out, sem):
    count = first_out.shape[0]
    low = pltpu.make_async_copy(first.at[pl.ds(0, count)], first_out, sem.at[0])
    high = pltpu.make_async_copy(second.at[pl.ds(count, count)], second_out, sem.at[1])
    low.start()
    high.start()
    low.wait()
    high.wait()


def halves(first, second):
    block = (first.shape[0] // 2,) + first.shape[1:]
    anywhere = pl.BlockSpec(memory_space=pl.ANY)
    return pl.pallas_call(
        halves_kernel,
        in_specs=[anywhere] * 2,
        out_specs=[anywhere] * 2,
        out_shape=[jax.ShapeDtypeStruct(block, first.dtype)] * 2,
        scratch_shapes=[pltpu.SemaphoreType.DMA((2,))],
        compiler_params=pltpu.CompilerParams(vmem_limit_bytes=SMALL_VMEM_BYTES),
        cost_estimate=pl.CostEstimate(flops=0, bytes_accessed=2_000_000, transcendentals=0),
        name="halves",
    )(first, second)


def ring(block, step):
    return lax.ppermute(block, "y", [(i, (i + step) % 4) for i in range(4)])


def per_device(
    activations,
    conditioning,
    pair_features,
    key_mask,
    w_scale,
    w_shift,
    w_query,
    w_key,
    w_value,
    w_gate,
    w_out,
    w_outgate,
    w_bias,
):
    tokens = activations.shape[1]
    kv, q, modulated, cond_norm = project_qkv(
        activations, conditioning, key_mask.reshape(1, tokens), w_scale, w_shift, w_query, w_key, w_value
    )
    exchange = lambda a: lax.all_to_all(a, XZ, 0, 0, tiled=True)
    bias = project_bias(pair_features, w_bias.T, q)
    kv, bias = lax.optimization_barrier((exchange(kv), bias))
    up, down = ring(kv, 1), ring(kv, 3)
    own = exchange(bias)
    gate, out_gate = gates(modulated, cond_norm, placement(), w_gate, w_outgate)
    up, down, gate, out_gate = lax.optimization_barrier((up, down, gate, out_gate))
    up_half, down_half = halves(up, down)
    far = (ring(up_half, 1), ring(down_half, 3))
    other = lax.ppermute(own, "co", [(0, 1), (1, 0)])
    place = jnp.stack([lax.axis_index("co"), lax.axis_index("y")]).astype(jnp.int32)
    kv = [a.reshape(-1, 4, 2, tokens, kv.shape[-1]) for a in (kv, up, *far, down)]
    own, other = (a.reshape(8, 2, tokens, own.shape[-1]) for a in (own, other))
    attended = attend(lay_keys(place, kv), own, other)
    attended = exchange(attended.reshape(HEADS, tokens, 2 * LANES))
    return project_out(attended, gate, out_gate, activations, w_out)


def solution(mesh):
    fine = Mesh(mesh.devices.reshape(2, 4, 4, 2, 2), ("zh", "x", "y", "zl", "co"))
    wide, narrow = ("zh", "x", "y"), ("zl", "co")
    in_specs = (
        P(narrow, wide, None),
        P(narrow, wide, None),
        P(wide, narrow, None),
        P(wide),
    ) + (P(),) * 9
    return jax.shard_map(
        per_device, mesh=fine, in_specs=in_specs, out_specs=P(narrow, wide, None), check_vma=False
    )
```

```python
import math

import jax
import jax.numpy as jnp
import numpy as np
from jax import lax
from jax.experimental import pallas as pl
from jax.experimental.pallas import tpu as pltpu
from jax.sharding import Mesh, PartitionSpec as P

EPSILON = 1e-05
NEGATIVE = -1e30
LOG2E = math.log2(math.e)
HEADS = 16
HEAD = 48
LANES = 128
GROUP = 16
MARK_LANE = 95
PAD_LANE = 96
SUM_LANE = 97
XZ = ("zh", "x", "zl")
BF = jnp.bfloat16
F32 = jnp.float32
VMEM_BYTES = 56 * 1024 * 1024
SMALL_VMEM_BYTES = 40 * 1024 * 1024
NT = (((1,), (1,)), ((), ()))


def layer_norm(entries):
    entries = entries.astype(F32)
    row_mean = jnp.mean(entries, axis=-1, keepdims=True)
    centered = entries - row_mean
    variance = jnp.mean(centered * centered, axis=-1, keepdims=True)
    return centered * lax.rsqrt(variance + EPSILON)


def dot(left, right):
    return jnp.dot(left, right, preferred_element_type=F32)


def placement():
    pairs = np.zeros((HEADS // 2, 2 * HEAD, HEADS // 2, LANES), np.float32)
    for pair in range(HEADS // 2):
        for channel in range(2 * HEAD):
            pairs[pair, channel, pair, channel] = 1
    return jnp.asarray(pairs.reshape(HEADS * HEAD, HEADS // 2 * LANES), BF)


def moved(columns, rows, head, to, lane):
    tile, offset = divmod(head * HEAD, LANES)
    shift = (to - offset) % LANES
    take = lambda i: columns[rows, i * LANES:(i + 1) * LANES]
    turn = lambda x: pltpu.roll(x, shift, axis=1) if shift else x
    first = turn(take(tile))
    if offset + HEAD <= LANES:
        return first
    return jnp.where(lane < to + LANES - offset, first, turn(take(tile + 1)))


def qkv_kernel(act, cond, mask, ws, wsh, wq, wk, wv, kv_out, q_out, mod_out, cn_out, mod):
    samples, tokens, width = act.shape
    rows = samples * tokens

    @pl.when(pl.program_id(0) == 0)
    def _():
        cond_norm = layer_norm(cond[...].reshape(rows, cond.shape[2])).astype(BF)
        normed = layer_norm(act[...].reshape(rows, width))
        modulated = jax.nn.sigmoid(dot(cond_norm, ws[...])) * normed + dot(cond_norm, wsh[...])
        mod[...] = modulated.astype(BF)
        mod_out[...] = mod[...].reshape(mod_out.shape)
        cn_out[...] = cond_norm.reshape(cn_out.shape)

    modulated = mod[...]
    lane = lax.broadcasted_iota(jnp.int32, (tokens, LANES), 1)
    square = (tokens, tokens)
    diagonal = lax.broadcasted_iota(jnp.int32, square, 0) == lax.broadcasted_iota(jnp.int32, square, 1)
    padded = jnp.broadcast_to(jnp.where(mask[...] > 0, 0.0, 1.0), square)
    padded = jnp.sum(jnp.where(diagonal, padded, 0.0), axis=1, keepdims=True)
    marked = (lane == MARK_LANE) & (padded > 0.5)
    sample = [slice(s * tokens, (s + 1) * tokens) for s in range(samples)]
    k = dot(modulated, wk[...])
    v = dot(modulated, wv[...])
    for h in range(GROUP):
        tile = [
            jnp.where(lane < HEAD, moved(k, row, h, 0, lane), moved(v, row, h, HEAD, lane)) for row in sample
        ]
        for s in range(3):
            spare = pltpu.roll(tile[3], 96 - 32 * s, axis=1)
            merged = jnp.where(lane < 96, tile[s], spare)
            if s == 0:
                merged = jnp.where(marked, NEGATIVE, merged)
            kv_out[h, :, s * LANES:(s + 1) * LANES] = merged.astype(BF)
    q = dot(modulated, wq[...]) * (LOG2E / math.sqrt(HEAD))
    for h in range(GROUP):
        for p in range(samples // 2):
            first = moved(q, sample[2 * p], h, 0, lane)
            second = moved(q, sample[2 * p + 1], h, 64, lane)
            q_out[h, :, p * LANES:(p + 1) * LANES] = jnp.where(lane < 64, first, second).astype(BF)


def project_qkv(act, cond, mask, ws, wsh, wq, wk, wv):
    samples, tokens, width = act.shape
    steps = HEADS // GROUP
    columns = GROUP * HEAD
    whole = lambda a: pl.BlockSpec(a.shape, lambda g: (0,) * a.ndim)
    part = pl.BlockSpec((width, columns), lambda g: (0, g))
    return pl.pallas_call(
        qkv_kernel,
        grid=(steps,),
        in_specs=[whole(act), whole(cond), whole(mask), whole(ws), whole(wsh), part, part, part],
        out_specs=[
            pl.BlockSpec((GROUP, tokens, 3 * LANES), lambda g: (g, 0, 0)),
            pl.BlockSpec((GROUP, tokens, 2 * LANES), lambda g: (g, 0, 0)),
            whole(act),
            whole(cond),
        ],
        out_shape=[
            jax.ShapeDtypeStruct((HEADS, tokens, 3 * LANES), BF),
            jax.ShapeDtypeStruct((HEADS, tokens, 2 * LANES), BF),
            jax.ShapeDtypeStruct(act.shape, BF),
            jax.ShapeDtypeStruct(cond.shape, BF),
        ],
        scratch_shapes=[pltpu.VMEM((samples * tokens, width), BF)],
        compiler_params=pltpu.CompilerParams(vmem_limit_bytes=VMEM_BYTES),
        cost_estimate=pl.CostEstimate(flops=4_000_000_000, bytes_accessed=10_000_000, transcendentals=300_000),
        name="qkv",
    )(act, cond, mask, ws, wsh, wq, wk, wv)


def bias_kernel(pair, w_bias, q, out, rows):
    count, keys, channels = pair.shape
    wt = w_bias[...]
    zero = jnp.zeros((HEADS, channels), BF)
    part = jnp.full((HEADS, channels), 1.0 / channels, BF)
    weights = jnp.concatenate(
        [jnp.concatenate([wt, zero], axis=1), jnp.concatenate([zero, part], axis=1)], axis=0
    )
    for i in range(count):
        x = pair[i].astype(F32)
        c = (x - jnp.mean(x, axis=1, keepdims=True)).astype(BF)
        both = jnp.concatenate([c, c * c], axis=1)
        r = lax.dot_general(weights, both, NT, preferred_element_type=F32)
        rows[i] = r[:HEADS] * (lax.rsqrt(r[HEADS:] + EPSILON) * LOG2E)
    out[:, :, :keys] = jnp.swapaxes(rows[...], 0, 1).astype(BF)
    out[:, :, keys:] = q[...]


def project_bias(pair, w_bias, q):
    queries, keys, channels = pair.shape
    step = 16
    extent = keys + q.shape[2]
    return pl.pallas_call(
        bias_kernel,
        grid=(queries // step,),
        in_specs=[
            pl.BlockSpec((step, keys, channels), lambda i: (i, 0, 0)),
            pl.BlockSpec(w_bias.shape, lambda i: (0, 0)),
            pl.BlockSpec((HEADS, step, q.shape[2]), lambda i: (0, i, 0)),
        ],
        out_specs=pl.BlockSpec((HEADS, step, extent), lambda i: (0, i, 0)),
        out_shape=jax.ShapeDtypeStruct((HEADS, queries, extent), BF),
        scratch_shapes=[pltpu.VMEM((step, HEADS, keys), F32)],
        compiler_params=pltpu.CompilerParams(vmem_limit_bytes=VMEM_BYTES),
        cost_estimate=pl.CostEstimate(flops=10_000_000_000, bytes_accessed=15_000_000, transcendentals=100_000),
        name="bias",
    )(pair, w_bias, q)


T = 4
PIECE = 128
LIMIT = 2.0**100


def lay_kernel(place, near, up, far_low, far_high, down, keys):
    tokens = near.shape[-2]
    core, row = place[0], place[1]
    lane = lax.broadcasted_iota(jnp.int32, (tokens, LANES), 1)
    for z in range(2):
        parts = (near.at[z], up.at[z], (far_low, far_high)[z].at[0], down.at[z])
        for o in range(2):
            quarter = core if o == 0 else 1 - core
            for low in range(2):
                for step, part in enumerate(parts):
                    block = (z * 2 + o) * 8 + low * 4 + lax.rem(row + 4 - step, 4)
                    at = pl.ds(pl.multiple_of(block * tokens, 16), tokens)
                    tiles = [part[2 * quarter + low, 0, :, i * LANES:(i + 1) * LANES] for i in range(3)]
                    wide = [t.astype(F32) for t in tiles]
                    mark = pltpu.roll(wide[0], PAD_LANE - MARK_LANE, axis=1)
                    pad = jnp.where(mark < 0.5 * NEGATIVE, NEGATIVE, 0.0)
                    tail = jnp.where(lane == PAD_LANE, pad, jnp.where(lane == SUM_LANE, 1.0, 0.0)).astype(BF)
                    for s in range(3):
                        keys[0, s, at] = jnp.where(lane < 96, tiles[s], tail)
                    last = jnp.where(
                        lane < 32,
                        pltpu.roll(wide[0], 32, axis=1),
                        jnp.where(lane < 64, pltpu.roll(wide[1], 64, axis=1), pltpu.roll(wide[2], 96, axis=1)),
                    ).astype(BF)
                    keys[0, 3, at] = jnp.where(lane < 96, last, tail)


def lay_keys(place, kv):
    tokens = kv[0].shape[3]
    extent = 32 * tokens
    return pl.pallas_call(
        lay_kernel,
        grid_spec=pltpu.PrefetchScalarGridSpec(
            num_scalar_prefetch=1,
            grid=(2,),
            in_specs=[pl.BlockSpec((a.shape[0], 4, 1, tokens, 3 * LANES), lambda z, c: (0, 0, z, 0, 0)) for a in kv],
            out_specs=pl.BlockSpec((1, 4, extent, LANES), lambda z, c: (z, 0, 0, 0)),
        ),
        out_shape=jax.ShapeDtypeStruct((2, 4, extent, LANES), BF),
        compiler_params=pltpu.CompilerParams(vmem_limit_bytes=SMALL_VMEM_BYTES),
        cost_estimate=pl.CostEstimate(flops=40_000_000_000, bytes_accessed=10_000_000, transcendentals=0),
        name="lay",
    )(place, *kv)


def attend_kernel(q, keys, own, other, out):
    tokens = q.shape[2]
    chunk = 8 * tokens
    span = T * tokens
    lane = lax.broadcasted_iota(jnp.int32, (span, LANES), 1)
    pad_one = jnp.where(lane == PAD_LANE, 1.0, 0.0).astype(BF)

    def query(t, s):
        pair_q = q[pl.ds(t * T, T), 0].reshape(span, LANES)
        if s == 1:
            pair_q = pltpu.roll(pair_q.astype(F32), 64, axis=1).astype(BF)
        return jnp.where(lane < HEAD, pair_q, pad_one)

    def scores(mine, t, s, at, width):
        part = lax.dot_general(mine, keys[0, s, at:at + width], NT, preferred_element_type=F32)
        columns = at % chunk
        bias = own if at // chunk % 2 == 0 else other
        bias = bias[pl.ds(t * T, T), at // chunk // 2, :, columns:columns + width].reshape(span, width)
        return part + bias.astype(F32)

    def values(p, s, at, width):
        return dot(p, keys[0, s, at:at + width])

    def store(t, pair):
        low = pltpu.roll(pair[0], LANES - HEAD, axis=1)
        high = pltpu.roll(pair[1], 64 - HEAD, axis=1)
        merged = jnp.where(lane < 64, low, high).astype(BF)
        out[pl.ds(t * T, T), 0] = merged.reshape(T, tokens, LANES)

    pieces = [(t, s, at) for t in range(8 // T) for s in range(2) for at in range(0, 4 * chunk, PIECE)]
    mine = {block: query(*block) for block in {piece[:2]: None for piece in pieces}}
    following = scores(mine[pieces[0][:2]], *pieces[0], PIECE)
    top, total, pair, worst = None, None, [], jnp.float32(0.0)
    for i, (t, s, at) in enumerate(pieces):
        current = following
        if at == 0:
            top, total = jnp.max(current, axis=1, keepdims=True), None
        if i + 1 < len(pieces):
            following = scores(mine[pieces[i + 1][:2]], *pieces[i + 1], PIECE)
        part = values(jnp.exp2(current - top).astype(BF), s, at, PIECE)
        total = part if total is None else total + part
        if at == 4 * chunk - PIECE:
            weight = total[:, SUM_LANE:SUM_LANE + 1]
            worst = jnp.maximum(worst, jnp.max(weight))
            pair.append(total / weight)
            if s == 1:
                store(t, pair)
                pair = []

    @pl.when(jnp.logical_not(worst < LIMIT))
    def _():
        def block(t, carried):
            pair = []
            for s in range(2):
                top = total = None
                row = query(t, s)
                for at in range(0, 4 * chunk, chunk):
                    peak = jnp.max(scores(row, t, s, at, chunk), axis=1, keepdims=True)
                    top = peak if top is None else jnp.maximum(top, peak)
                for at in range(0, 4 * chunk, chunk):
                    p = jnp.exp2(scores(row, t, s, at, chunk) - top).astype(BF)
                    part = values(p, s, at, chunk)
                    total = part if total is None else total + part
                pair.append(total / total[:, SUM_LANE:SUM_LANE + 1])
            store(t, pair)
            return carried

        lax.fori_loop(0, 8 // T, block, 0)


def attend(keys, own, other):
    tokens = own.shape[2]
    chunk = 8 * tokens
    b_spec = pl.BlockSpec(memory_space=pltpu.VMEM)
    return pl.pallas_call(
        attend_kernel,
        grid=(2, 2),
        in_specs=[
            pl.BlockSpec((8, 1, tokens, LANES), lambda z, p: (0, z, 0, chunk // LANES + p)),
            pl.BlockSpec((1, 2, 4 * chunk, LANES), lambda z, p: (z, p, 0, 0)),
            b_spec,
            b_spec,
        ],
        out_specs=pl.BlockSpec((8, 1, tokens, LANES), lambda z, p: (0, z, 0, p)),
        out_shape=jax.ShapeDtypeStruct((8, 2, tokens, 2 * LANES), BF),
        compiler_params=pltpu.CompilerParams(vmem_limit_bytes=SMALL_VMEM_BYTES),
        cost_estimate=pl.CostEstimate(flops=14_000_000_000, bytes_accessed=10_000_000, transcendentals=13_000_000),
        name="attend",
    )(own, keys, own, other)


def gate_kernel(mod, cn, place, wg, wog, gate_out, og_out):
    samples, tokens, width = mod.shape
    rows = samples * tokens
    og_out[...] = jax.nn.sigmoid(dot(cn[...].reshape(rows, cn.shape[2]), wog[...])).reshape(og_out.shape)
    placed = dot(wg[...], place[...]).astype(BF)
    gate = jax.nn.sigmoid(dot(mod[...].reshape(rows, width), placed))
    gate_out[...] = gate.reshape(gate_out.shape)


def gates(mod, cn, place, wg, wog):
    samples, tokens, width = mod.shape
    return pl.pallas_call(
        gate_kernel,
        out_shape=[
            jax.ShapeDtypeStruct((samples, tokens, HEADS // 2 * LANES), F32),
            jax.ShapeDtypeStruct(mod.shape, F32),
        ],
        compiler_params=pltpu.CompilerParams(vmem_limit_bytes=SMALL_VMEM_BYTES),
        cost_estimate=pl.CostEstimate(flops=32_000_000_000, bytes_accessed=9_000_000, transcendentals=1_000_000),
        name="gates",
    )(mod, cn, place, wg, wog)


def out_kernel(attended, gate, og, act, wo, out, table):
    samples, tokens, width = act.shape
    table[...] = jnp.zeros_like(table)
    for j in range(HEADS // 2):
        table[j * LANES:j * LANES + 96] = wo[j * 96:(j + 1) * 96]
    lane = lax.broadcasted_iota(jnp.int32, (tokens, LANES), 1)
    rows = []
    for s in range(samples):
        lanes = slice(s // 2 * LANES, (s // 2 + 1) * LANES)
        tiles = []
        for j in range(HEADS // 2):
            first = attended[2 * j, :, lanes].astype(F32)
            second = attended[2 * j + 1, :, lanes].astype(F32)
            if s % 2 == 0:
                second = pltpu.roll(second, HEAD, axis=1)
            else:
                first = pltpu.roll(first, 64, axis=1)
                second = pltpu.roll(second, 64 + HEAD, axis=1)
            both = jnp.where(lane < HEAD, first, second)
            tiles.append((both * gate[s, :, j * LANES:(j + 1) * LANES]).astype(BF))
        rows.append(jnp.concatenate(tiles, axis=1))
    projected = dot(jnp.concatenate(rows, axis=0), table[...])
    out[...] = (act[...].astype(F32) + og[...] * projected.reshape(act.shape)).astype(BF)


def project_out(attended, gate, og, act, wo):
    width = act.shape[2]
    return pl.pallas_call(
        out_kernel,
        out_shape=jax.ShapeDtypeStruct(act.shape, BF),
        scratch_shapes=[pltpu.VMEM((HEADS // 2 * LANES, width), BF)],
        compiler_params=pltpu.CompilerParams(vmem_limit_bytes=SMALL_VMEM_BYTES),
        cost_estimate=pl.CostEstimate(flops=2_000_000_000, bytes_accessed=6_000_000, transcendentals=0),
        name="out",
    )(attended, gate, og, act, wo)


def halves_kernel(first, second, first_out, second_out):
    first_out[...] = first[...]
    second_out[...] = second[...]


def halves(first, second):
    block = (first.shape[0] // 2,) + first.shape[1:]
    low = pl.BlockSpec(block, lambda i: (0, 0, 0))
    high = pl.BlockSpec(block, lambda i: (1, 0, 0))
    return pl.pallas_call(
        halves_kernel,
        grid=(1,),
        in_specs=[low, high],
        out_specs=[low, low],
        out_shape=[jax.ShapeDtypeStruct(block, first.dtype)] * 2,
        compiler_params=pltpu.CompilerParams(vmem_limit_bytes=SMALL_VMEM_BYTES),
        cost_estimate=pl.CostEstimate(flops=0, bytes_accessed=2_000_000, transcendentals=0),
        name="halves",
    )(first, second)


def ring(block, step):
    return lax.ppermute(block, "y", [(i, (i + step) % 4) for i in range(4)])


def per_device(
    activations,
    conditioning,
    pair_features,
    key_mask,
    w_scale,
    w_shift,
    w_query,
    w_key,
    w_value,
    w_gate,
    w_out,
    w_outgate,
    w_bias,
):
    tokens = activations.shape[1]
    kv, q, modulated, cond_norm = project_qkv(
        activations, conditioning, key_mask.reshape(1, tokens), w_scale, w_shift, w_query, w_key, w_value
    )
    exchange = lambda a: lax.all_to_all(a, XZ, 0, 0, tiled=True)
    bias = project_bias(pair_features, w_bias.T, q)
    kv, bias = lax.optimization_barrier((exchange(kv), bias))
    up, down = ring(kv, 1), ring(kv, 3)
    own = exchange(bias)
    gate, out_gate = gates(modulated, cond_norm, placement(), w_gate, w_outgate)
    up, down, gate, out_gate = lax.optimization_barrier((up, down, gate, out_gate))
    up_half, down_half = halves(up, down)
    far = (ring(up_half, 1), ring(down_half, 3))
    other = lax.ppermute(own, "co", [(0, 1), (1, 0)])
    place = jnp.stack([lax.axis_index("co"), lax.axis_index("y")]).astype(jnp.int32)
    kv = [a.reshape(-1, 4, 2, tokens, kv.shape[-1]) for a in (kv, up, *far, down)]
    own, other = (a.reshape(8, 2, tokens, own.shape[-1]) for a in (own, other))
    attended = attend(lay_keys(place, kv), own, other)
    attended = exchange(attended.reshape(HEADS, tokens, 2 * LANES))
    return project_out(attended, gate, out_gate, activations, w_out)


def solution(mesh):
    fine = Mesh(mesh.devices.reshape(2, 4, 4, 2, 2), ("zh", "x", "y", "zl", "co"))
    wide, narrow = ("zh", "x", "y"), ("zl", "co")
    in_specs = (
        P(narrow, wide, None),
        P(narrow, wide, None),
        P(wide, narrow, None),
        P(wide),
    ) + (P(),) * 9
    return jax.shard_map(
        per_device, mesh=fine, in_specs=in_specs, out_specs=P(narrow, wide, None), check_vma=False
    )
```
